32 devices in a mesh: req: 4 (over z), exp: 8 (over y, x, core).
Axes of the slice: x: 2, y: 2, z: 4, core: 2. Of those that a mesh axis runs over, the one named last changes fastest.
Arguments:
- hidden: bfloat16 [4096, 2048], P(('req', 'exp')), may hold values from -6 to 6
- attn_gain: float32 [2048], replicated, may hold values from 0.5 to 1.5
- w_query: bfloat16 [2048, 1024], P(None, 'exp'), may hold values from -0.125 to 0.125
- w_keyval: bfloat16 [2, 2048, 1024], P(None, None, 'exp'), may hold values from -0.3125 to 0.3125
- k_pool: bfloat16 [640, 128, 1024], P('req', None, 'exp'), may hold values from -86 to 86
- v_pool: bfloat16 [640, 128, 1024], P('req', None, 'exp'), may hold values from -16 to 16
- dec_len: int32 [16], P('req'), may hold values from 1 to 4096, as said below
- dec_pages: int32 [16, 32], P('req'), may hold values from 0 to 159, as said below
- pre_pos: int32 [4], P('req'), may hold values from 0 to 4096, as said below
- pre_pages: int32 [4, 32], P('req'), may hold values from 0 to 159
- w_out: bfloat16 [1024, 2048], P('exp'), may hold values from -0.1875 to 0.1875
- moe_gain: float32 [2048], replicated, may hold values from 0.1 to 1.9
- expert_ids: int32 [4096, 8], P(('req', 'exp')), may hold values from 0 to 15, all different within a row; in each aligned block of 128 rows (0 to 127, 128 to 255, ...) at most 80 rows name the same one
- router_logits: float32 [4096, 8], P(('req', 'exp')), may hold values from -0.4 to 283
- w_in: bfloat16 [32, 2048, 1024], P(('req', 'exp')), may hold values from -0.125 to 0.125
- w_down: bfloat16 [32, 512, 2048], P(('req', 'exp')), may hold values from -0.25 to 0.25
Outputs:
- mixed: bfloat16 [4096, 2048], P(('req', 'exp'))
- new_kv: bfloat16 [2, 4096, 1024], P(None, 'req', 'exp')
The draws below stay inside these ranges and needn't reach their ends.
Inputs may be any that keep to these rules, and one draw needn't show every extreme that they name: Within each group, the rows of dec_pages of its 4 requests and its row of pre_pages name every one of the group's 160 pages exactly once. `dec_len`: some request has exactly 4096 cached positions. `pre_pos`: some group's prefix has exactly 4096 positions. `expert_ids`: each row names 8 different experts; among the rows of one device no expert is named by more than 80 rows.
All inputs are finite; a program needn't handle non-finite values.
Results may differ from the reference program's by a relative error of at most 0.02.
Values may be sent and summed in bfloat16 or wider, within the bound.
No kernel may reach another device: no remote copies, remote signals or barrier semaphores. Data moves between devices by JAX's collectives and lax.ppermute only.
A program may use at most 128 MiB of HBM per device.

```python
import math
import jax
import jax.numpy as jnp
import numpy as np
from jax import lax

D = 2048
HD = 128
FF = 1024
TOPK = 8
SPLIT = 2
PAGE = 128
DEC_GRP = 4
DEC_PAGES = 32
TOK_DEV = 128
HEADS = 8
EXPERTS = 16
CAP = 80
TOKENS = 4096
PAGES = 160
DEC_MAX = 4096
PRE_MAX = 4096
N_REQ = 4
N_EXP = 8


def pool_tables(key):

    def one_group(group):
        return jax.random.permutation(jax.random.fold_in(key, group), PAGES).astype(jnp.int32)
    return jax.vmap(one_group)(jnp.arange(N_REQ, dtype=jnp.int32))


def draw_dec_pages(key, part):
    tables = pool_tables(jax.random.fold_in(key, 11))
    return tables[:, :DEC_GRP * DEC_PAGES].reshape(N_REQ * DEC_GRP, DEC_PAGES)


def draw_pre_pages(key, part):
    tables = pool_tables(jax.random.fold_in(key, 11))
    return tables[:, DEC_GRP * DEC_PAGES:]


def draw_dec_len(key, part):
    first, second = jax.random.split(jax.random.fold_in(key, 21))
    lengths = jax.random.randint(first, (N_REQ * DEC_GRP,), 1, DEC_MAX + 1)
    where = jax.random.randint(second, (), 0, N_REQ * DEC_GRP)
    return lengths.at[where].set(DEC_MAX).astype(jnp.int32)


def draw_pre_pos(key, part):
    first, second = jax.random.split(jax.random.fold_in(key, 23))
    starts = jax.random.randint(first, (N_REQ,), 0, PRE_MAX + 1)
    where = jax.random.randint(second, (), 0, N_REQ)
    return starts.at[where].set(PRE_MAX).astype(jnp.int32)


def draw_k_pool(key, part):
    first = jax.random.fold_in(jax.random.fold_in(key, 31), 0)
    shape = (N_REQ * PAGES, PAGE, HEADS * HD)
    return (jnp.clip(jax.random.normal(first, shape, jnp.float32), -6.0, 6.0) * 2.5).astype(jnp.bfloat16)


def draw_router_logits(key, part):
    first = jax.random.fold_in(jax.random.fold_in(key, 41), 0)
    shape = (TOKENS, TOPK)
    return jax.random.uniform(first, shape, jnp.float32, -0.4, 0.4)


def block_levels(stream_key, dims, cuts, least, top_value):
    level = 1.0
    for axis_at, parts in cuts:
        draws = jax.random.uniform(jax.random.fold_in(jax.random.fold_in(stream_key, 6), axis_at), (parts,), jnp.float32, least / len(cuts), top_value / len(cuts))
        level = level * jnp.repeat(jnp.exp(draws), dims[axis_at] // parts).reshape((-1,) + (1,) * (len(dims) - 1 - axis_at))
    return level


def assign_block(key, own, number, rows, count, top, most, skew):
    order = jax.random.permutation(key, count)
    heavy_load, ordinary = shares(count, rows * top, most, skew, True), shares(count, rows * top, most, skew, False)
    places = jnp.arange(count)

    def named(tallies, rotation):
        used = int((tallies > 0).sum())
        fixed = max(1, used // 4)
        shifted = fixed + (places - fixed + rotation * (used - fixed)) % max(1, count - fixed)
        return jnp.zeros((count,), jnp.int32).at[order[jnp.where(places < fixed, places, shifted)]].set(jnp.asarray(tallies, jnp.int32))

    tallies = jnp.where(number % 4 == 0, named(heavy_load, number // 4), named(ordinary, number - number // 4 - 1))
    mixed = jax.random.permutation(jax.random.fold_in(own, 3), count)
    donor, taker = mixed[0:count // 2 * 2:2], mixed[1:count // 2 * 2:2]
    room = jnp.minimum(tallies[donor] - 1, most - tallies[taker]) // 2
    room = jnp.where((donor == order[0]) | (taker == order[0]) | (tallies[taker] == 0), 0, jnp.maximum(room, 0))
    shifted = jax.random.randint(jax.random.fold_in(own, 4), (count // 2,), 0, 1 << 20) % (room + 1)
    tallies = tallies.at[donor].add(-shifted).at[taker].add(shifted)
    members = jnp.searchsorted(jnp.cumsum(tallies), jnp.arange(rows * top), side="right").astype(jnp.int32)
    listing = members.reshape(top, rows).T
    listing = listing[jax.random.permutation(jax.random.fold_in(own, 1), rows)]
    rotation = jax.random.randint(jax.random.fold_in(own, 2), (rows, 1), 0, top)
    return jnp.take_along_axis(listing, (jnp.arange(top)[None, :] + rotation) % top, axis=1)


def shares(count, total, reach, skew, full):
    portions = [(1 << 20) // math.isqrt(grade ** skew) + 1 for grade in range(1, count + 1)]
    largest = reach if full else min(reach, max(-(-total // count), total * portions[0] // sum(portions)))
    least = 1 if total - largest >= count - 1 else 0
    holding, spare = [largest] + [least] * (count - 1), total - largest - least * (count - 1)
    while spare > 0:
        free = [i for i in range(1, count) if holding[i] < largest] or [i for i in range(1, count) if holding[i] < reach]
        pool, remaining = sum([portions[i] for i in free]), spare
        for i in free:
            extra = min(reach - holding[i], max(1, remaining * portions[i] // pool), spare)
            holding[i] = holding[i] + extra
            spare = spare - extra
    return np.array(holding)


def noise(key, dims, spread, reach, pieces=(), kind=jnp.bfloat16):
    loudness = block_levels(key, dims, pieces, -0.22, 0.18) if pieces else 1.0
    values = jax.random.normal(key, dims, jnp.float32) * spread * loudness
    return jnp.minimum(jnp.maximum(values, -reach), reach).astype(kind)


def setup_inputs(seed: int = 0) -> dict:
    key_of = jax.random.split(jax.random.key(seed), 17)
    hidden = noise(key_of[0], (TOKENS, D), 1.0, 6.0, ((0, 32),))
    attn_gain = jnp.clip(1.0 + 0.1 * jax.random.normal(key_of[1], (D,), jnp.float32), 0.5, 1.5)
    w_query = noise(key_of[2], (D, HEADS * HD), D ** -0.5, 0.125, ((1, 8),))
    w_keyval = noise(key_of[3], (2, D, HEADS * HD), (2.5 * D ** -0.5), 0.3125, ((2, 8),))
    k_pool = draw_k_pool(jax.random.fold_in(key_of[16], 71), 0)
    v_pool = noise(key_of[5], (N_REQ * PAGES, PAGE, HEADS * HD), 2.5, 16.0, ((0, 4), (2, 8)))
    dec_len = draw_dec_len(jax.random.fold_in(key_of[16], 71), 0)
    dec_pages = draw_dec_pages(jax.random.fold_in(key_of[16], 71), 0)
    pre_pos = draw_pre_pos(jax.random.fold_in(key_of[16], 71), 0)
    pre_pages = draw_pre_pages(jax.random.fold_in(key_of[16], 71), 0)
    w_out = noise(key_of[10], (HEADS * HD, D), (HEADS * HD) ** -0.5, 0.1875, ((0, 8),))
    moe_gain = jnp.clip(1.0 + 0.18 * jax.random.normal(key_of[11], (D,), jnp.float32), 0.1, 1.9)
    expert_ids_keys = jax.random.split(jax.random.fold_in(key_of[12], 1), TOKENS // TOK_DEV)
    expert_ids_turns = jax.random.permutation(jax.random.fold_in(key_of[12], 3), TOKENS // TOK_DEV)
    expert_ids = jax.vmap(lambda own, number: assign_block(jax.random.fold_in(key_of[12], 2), own, number, TOK_DEV, EXPERTS, TOPK, CAP, 2))(expert_ids_keys, expert_ids_turns).reshape((TOKENS, TOPK))
    router_logits = draw_router_logits(jax.random.fold_in(key_of[16], 71), 0)
    w_in = noise(key_of[14], (EXPERTS * SPLIT, D, 2 * (FF // SPLIT)), D ** -0.5, 0.125, ((0, 32),))
    w_down = noise(key_of[15], (EXPERTS * SPLIT, FF // SPLIT, D), (FF // SPLIT) ** -0.5, 0.25, ((0, 32),))
    return {"hidden": hidden, "attn_gain": attn_gain, "w_query": w_query, "w_keyval": w_keyval, "k_pool": k_pool, "v_pool": v_pool, "dec_len": dec_len, "dec_pages": dec_pages, "pre_pos": pre_pos, "pre_pages": pre_pages, "w_out": w_out, "moe_gain": moe_gain, "expert_ids": expert_ids, "router_logits": router_logits, "w_in": w_in, "w_down": w_down}


EPSILON = 1e-05
THETA = 10000.0

def rms_scale(inputs, gain):
    values = inputs.astype(jnp.float32)
    mean_square = lax.optimization_barrier(jnp.mean(values * values, axis=-1, keepdims=True))
    return (values * lax.rsqrt(mean_square + EPSILON) * gain).astype(jnp.bfloat16)

def rotate(values, positions):
    head_size = values.shape[-1]
    half = head_size // 2
    steps = jnp.arange(half, dtype=jnp.float32)
    frequency = jnp.exp(steps * (-2.0 * math.log(THETA) / head_size))
    angles = positions.astype(jnp.float32)[:, None, None] * frequency[None, None, :]
    cosine = jnp.cos(angles)
    sine = jnp.sin(angles)
    first = values[..., :half]
    second = values[..., half:]
    return jnp.concatenate([first * cosine - second * sine, second * cosine + first * sine], axis=-1)

def attend(query, keys, values, allowed):
    scores = jnp.dot(query, keys.T, preferred_element_type=jnp.float32) * (1.0 / math.sqrt(query.shape[-1]))
    scores = jnp.where(allowed, scores, -jnp.inf)
    highest = lax.optimization_barrier(jnp.max(scores, axis=1, keepdims=True))
    weights = jnp.exp(scores - highest)
    total = lax.optimization_barrier(jnp.sum(weights, axis=1, keepdims=True))
    summed = jnp.dot(weights.astype(jnp.bfloat16), values, preferred_element_type=jnp.float32)
    return (summed / total).astype(jnp.bfloat16)

def reference(hidden, attn_gain, w_query, w_keyval, k_pool, v_pool, dec_len, dec_pages, pre_pos, pre_pages, w_out, moe_gain, expert_ids, router_logits, w_in, w_down):
    group_rows = TOK_DEV * N_EXP
    segment = group_rows - DEC_GRP
    normed_attn = rms_scale(hidden, attn_gain)
    row_index = jnp.arange(TOKENS, dtype=jnp.int32)
    group_of = row_index // group_rows
    inside = row_index % group_rows
    dec_index = group_of * DEC_GRP + jnp.minimum(inside, DEC_GRP - 1)
    positions = jnp.where(inside < DEC_GRP, dec_len[dec_index], pre_pos[group_of] + inside - DEC_GRP)
    query_all = jnp.dot(normed_attn, w_query, preferred_element_type=jnp.float32).reshape(TOKENS, HEADS, HD)
    keys_all = jnp.dot(normed_attn, w_keyval[0], preferred_element_type=jnp.float32).reshape(TOKENS, HEADS, HD)
    values_all = jnp.dot(normed_attn, w_keyval[1], preferred_element_type=jnp.float32).reshape(TOKENS, HEADS, HD)
    query = rotate(query_all, positions).astype(jnp.bfloat16)
    keys_new = rotate(keys_all, positions).astype(jnp.bfloat16)
    values_new = values_all.astype(jnp.bfloat16)
    new_kv = jnp.stack([keys_new.reshape(TOKENS, HEADS * HD), values_new.reshape(TOKENS, HEADS * HD)])

    def group_attention(group):
        start = group * group_rows
        query_group = lax.dynamic_slice_in_dim(query, start, group_rows, 0)
        keys_group = lax.dynamic_slice_in_dim(keys_new, start, group_rows, 0)
        values_group = lax.dynamic_slice_in_dim(values_new, start, group_rows, 0)
        pool_keys = lax.dynamic_slice_in_dim(k_pool, group * PAGES, PAGES, 0)
        pool_values = lax.dynamic_slice_in_dim(v_pool, group * PAGES, PAGES, 0)
        prefix_table = lax.dynamic_index_in_dim(pre_pages, group, 0, keepdims=False)
        length = lax.dynamic_index_in_dim(pre_pos, group, 0, keepdims=False)
        prefix_keys = pool_keys[prefix_table].reshape(PRE_MAX, HEADS, HD)
        prefix_values = pool_values[prefix_table].reshape(PRE_MAX, HEADS, HD)
        key_slots = jnp.arange(PRE_MAX, dtype=jnp.int32)
        own_slots = jnp.arange(segment, dtype=jnp.int32)
        allowed = jnp.concatenate([jnp.broadcast_to(key_slots[None, :] < length, (segment, PRE_MAX)), own_slots[None, :] <= own_slots[:, None]], axis=1)
        seg_query = query_group[DEC_GRP:]
        seg_keys = jnp.concatenate([prefix_keys, keys_group[DEC_GRP:]], axis=0)
        seg_values = jnp.concatenate([prefix_values, values_group[DEC_GRP:]], axis=0)

        def one_head(items):
            head_query, head_keys, head_values = items
            return attend(head_query, head_keys, head_values, allowed)
        seg_out = lax.map(one_head, (jnp.swapaxes(seg_query, 0, 1), jnp.swapaxes(seg_keys, 0, 1), jnp.swapaxes(seg_values, 0, 1)))
        seg_out = jnp.swapaxes(seg_out, 0, 1).reshape(segment, HEADS * HD)
        dec_tables = lax.dynamic_slice_in_dim(dec_pages, group * DEC_GRP, DEC_GRP, 0)
        dec_limits = lax.dynamic_slice_in_dim(dec_len, group * DEC_GRP, DEC_GRP, 0)
        cache_keys = pool_keys[dec_tables].reshape(DEC_GRP, DEC_MAX, HEADS, HD)
        cache_values = pool_values[dec_tables].reshape(DEC_GRP, DEC_MAX, HEADS, HD)

        def one_request(table_keys, table_values, own_query, own_key, own_value, limit):
            every_key = jnp.concatenate([table_keys, own_key[None]], axis=0)
            every_value = jnp.concatenate([table_values, own_value[None]], axis=0)
            visible = jnp.concatenate([jnp.arange(DEC_MAX, dtype=jnp.int32) < limit, jnp.array([True])])[None, :]
            per_head = jax.vmap(attend, in_axes=(0, 1, 1, None))(own_query[:, None, :], every_key, every_value, visible)
            return per_head.reshape(HEADS * HD)
        decode_out = jax.vmap(one_request)(cache_keys, cache_values, query_group[:DEC_GRP], keys_group[:DEC_GRP], values_group[:DEC_GRP], dec_limits)
        return jnp.concatenate([decode_out, seg_out], axis=0)
    attended = lax.map(group_attention, jnp.arange(N_REQ, dtype=jnp.int32)).reshape(TOKENS, HEADS * HD)
    projected = jnp.zeros((TOKENS, D), jnp.float32)
    for head in range(HEADS):
        term = jnp.dot(attended[:, head * HD:(head + 1) * HD], w_out[head * HD:(head + 1) * HD], preferred_element_type=jnp.float32)
        projected = projected + lax.optimization_barrier(term.astype(jnp.bfloat16)).astype(jnp.float32)
    residual = (hidden.astype(jnp.float32) + projected).astype(jnp.bfloat16)
    normed_moe = rms_scale(residual, moe_gain)
    gates = jax.nn.softmax(router_logits.astype(jnp.float32), axis=-1)
    flat_ids = expert_ids.reshape(-1)
    flat_gates = gates.reshape(-1)
    most = N_REQ * N_EXP * CAP
    piece_units = FF // SPLIT

    def one_piece(total, piece):
        expert = piece // SPLIT
        chosen = flat_ids == expert
        picked = jnp.nonzero(chosen, size=most, fill_value=0)[0].astype(jnp.int32)
        live = jnp.arange(most, dtype=jnp.int32) < jnp.sum(chosen.astype(jnp.int32))
        owners = picked // TOPK
        inputs = normed_moe[owners]
        inner = jnp.dot(inputs, w_in[piece], preferred_element_type=jnp.float32)
        activated = (jax.nn.silu(inner[:, :piece_units]) * inner[:, piece_units:]).astype(jnp.bfloat16)
        partial_value = jnp.dot(activated, w_down[piece], preferred_element_type=jnp.float32).astype(jnp.bfloat16)
        factor = jnp.where(live, flat_gates[picked], 0.0)
        total = total.at[owners].add(factor[:, None] * partial_value.astype(jnp.float32))
        return (total, None)
    moe_out = lax.scan(one_piece, jnp.zeros((TOKENS, D), jnp.float32), jnp.arange(EXPERTS * SPLIT, dtype=jnp.int32))[0]
    mixed = (residual.astype(jnp.float32) + moe_out).astype(jnp.bfloat16)
    return (mixed, new_kv)
```

```python
import math

import jax
import jax.numpy as jnp
from jax import lax
from jax.sharding import PartitionSpec as P

HD = 128
SPLIT = 2


EPSILON = 1e-05
THETA = 10000.0


def rms_scale(inputs, gain):
    values = inputs.astype(jnp.float32)
    mean_square = jnp.mean(values * values, axis=-1, keepdims=True)
    return (values * lax.rsqrt(mean_square + EPSILON) * gain).astype(jnp.bfloat16)


def rotate(values, positions):
    head_size = values.shape[-1]
    half = head_size // 2
    steps = jnp.arange(half, dtype=jnp.float32)
    frequency = jnp.exp(steps * (-2.0 * math.log(THETA) / head_size))
    angles = positions.astype(jnp.float32)[:, None, None] * frequency[None, None, :]
    cosine = jnp.cos(angles)
    sine = jnp.sin(angles)
    first = values[..., :half]
    second = values[..., half:]
    return jnp.concatenate(
        [first * cosine - second * sine, second * cosine + first * sine], axis=-1
    )


def online_block(state, query, keys, values, allowed, scale):
    old_max, old_total, running = state
    scores = jnp.einsum("qd,kd->qk", query, keys, preferred_element_type=jnp.float32) * scale
    scores = jnp.where(allowed, scores, -jnp.inf)
    new_max = jnp.maximum(old_max, jnp.max(scores, axis=1))
    anchor = jnp.where(jnp.isfinite(new_max), new_max, 0.0)
    shrink = jnp.exp(old_max - anchor)
    weights = jnp.exp(scores - anchor[:, None])
    new_total = old_total * shrink + jnp.sum(weights, axis=1)
    running = running * shrink[:, None] + jnp.dot(
        weights.astype(jnp.bfloat16), values, preferred_element_type=jnp.float32
    )
    return (new_max, new_total, running)


AXES = ("req", "exp")
WIDE = jnp.float32


def swap(values, bits):
    count = lax.axis_size("exp")
    return lax.ppermute(values, "exp", [(d, d ^ bits) for d in range(count)])


def shift(values, steps):
    count = lax.axis_size("req")
    return lax.ppermute(values, "req", [(d, (d + steps) % count) for d in range(count)])


def plane_gather(rows):
    half = rows.shape[0] // 2
    from_x = swap(rows, 2)
    from_y = swap(rows, 4)
    corner = [swap(from_x[:half], 4), swap(from_y[half:], 2)]
    return [rows, from_x, from_y, jnp.concatenate(corner, axis=0)]


def plane_reduce(parts):
    own, for_x, for_y, corner = parts
    half = own.shape[0] // 2
    via_x = swap(corner[:half], 2)
    via_y = swap(corner[half:], 4)
    sum_y = (for_y[:half].astype(WIDE) + via_x.astype(WIDE)).astype(own.dtype)
    sum_x = (for_x[half:].astype(WIDE) + via_y.astype(WIDE)).astype(own.dtype)
    back_y = swap(jnp.concatenate([sum_y, for_y[half:]], axis=0), 4)
    back_x = swap(jnp.concatenate([for_x[:half], sum_x], axis=0), 2)
    return own.astype(WIDE) + back_x.astype(WIDE) + back_y.astype(WIDE)


def dense_experts(normed_moe, gate_rows, w_in, w_down):
    own_in, own_down = w_in[0], w_down[0]
    pair_in, pair_down = swap(own_in, 1), swap(own_down, 1)
    units = own_down.shape[0]
    req_count = lax.axis_size("req")
    slots = []
    current = normed_moe
    for step in range(req_count):
        slots.append(plane_gather(current))
        if step + 1 < req_count:
            current = shift(current, 1)
    partials = []
    for step in range(req_count):
        rows = jnp.concatenate(slots[step], axis=0)
        total = 0.0
        for part_in, part_down in ((own_in, own_down), (pair_in, pair_down)):
            inner = jnp.dot(rows, part_in, preferred_element_type=WIDE)
            activated = (jax.nn.silu(inner[:, :units]) * inner[:, units:]).astype(jnp.bfloat16)
            total = total + jnp.dot(activated, part_down, preferred_element_type=WIDE)
        scaled = (total * gate_rows[step][:, None]).astype(jnp.bfloat16)
        partials.append(jnp.split(scaled, 4, axis=0))
    result = 0.0
    for step in list(range(1, req_count)) + [0]:
        reduced = plane_reduce(partials[step])
        if step:
            reduced = shift(reduced.astype(jnp.bfloat16), -step).astype(WIDE)
        result = result + reduced
    return result


def gate_table(expert_ids, gates):
    req_count = lax.axis_size("req")
    exp_count = lax.axis_size("exp")
    devices = req_count * exp_count
    experts = devices // SPLIT
    rows = expert_ids.shape[0]
    named = expert_ids[:, :, None] == jnp.arange(experts, dtype=jnp.int32)
    table = jnp.sum(jnp.where(named, gates[:, :, None], 0.0), axis=1)
    table = lax.all_gather(table, AXES, axis=0, tiled=True).reshape(devices, rows, experts)
    group = lax.axis_index("req")
    place = lax.axis_index("exp")
    mine = (group * exp_count + place) // SPLIT
    column = jnp.sum(jnp.where(jnp.arange(experts) == mine, table, 0.0), axis=-1)
    steps = jnp.arange(req_count, dtype=jnp.int32)[:, None]
    bits = jnp.arange(0, exp_count, 2, dtype=jnp.int32)[None, :]
    source = ((group - steps) % req_count) * exp_count + (place ^ bits)
    chosen = source[:, :, None] == jnp.arange(devices, dtype=jnp.int32)
    picked = jnp.sum(jnp.where(chosen[..., None], column[None, None], 0.0), axis=2)
    return picked.reshape(req_count, -1)


def deliver(buffer):
    result = lax.all_to_all(buffer, ("req", "exp"), split_axis=0, concat_axis=0, tiled=True)
    return result


def bring_back(buffer):
    result = lax.all_to_all(buffer, ("req", "exp"), split_axis=0, concat_axis=0, tiled=True)
    return result


def sparse_experts(normed_moe, expert_ids, gates, w_in, w_down):
    local_rows, width = normed_moe.shape
    devices = lax.axis_size("req") * lax.axis_size("exp")
    experts = devices // SPLIT
    top = expert_ids.shape[1]
    capacity = 2 * ((local_rows * top * 5 + 8 * experts - 1) // (8 * experts))
    assigned = expert_ids.reshape(-1)
    count_all = assigned.shape[0]
    marks = (assigned[:, None] == jnp.arange(experts, dtype=jnp.int32)[None, :]).astype(jnp.int32)
    earlier = jnp.cumsum(marks, axis=0) - marks
    place = jnp.sum(earlier * marks, axis=1)
    target = assigned * capacity + place
    owner_rows = jnp.arange(count_all, dtype=jnp.int32) // top
    outgoing = (
        jnp.zeros((experts * capacity, width), jnp.bfloat16).at[target].set(normed_moe[owner_rows])
    )
    doubled = jnp.broadcast_to(
        outgoing.reshape(experts, 1, capacity, width), (experts, SPLIT, capacity, width)
    ).reshape(devices, capacity, width)
    arrived = deliver(doubled)
    piece_units = w_down.shape[1]
    inner = jnp.dot(
        arrived.reshape(devices * capacity, width), w_in[0], preferred_element_type=jnp.float32
    )
    activated = (jax.nn.silu(inner[:, :piece_units]) * inner[:, piece_units:]).astype(jnp.bfloat16)
    partial_value = (
        jnp.dot(activated, w_down[0], preferred_element_type=jnp.float32)
        .astype(jnp.bfloat16)
        .reshape(devices, capacity, width)
    )
    returned = bring_back(partial_value).reshape(devices * capacity, width)
    base_index = assigned * (SPLIT * capacity) + place
    lower_half = returned[base_index].astype(jnp.float32)
    upper_half = returned[base_index + capacity].astype(jnp.float32)
    weighted = (lower_half + upper_half) * gates.reshape(-1)[:, None]
    moe_out = jnp.sum(weighted.reshape(local_rows, top, width), axis=1)
    return moe_out


def body(
    hidden,
    attn_gain,
    w_query,
    w_keyval,
    k_pool,
    v_pool,
    dec_len,
    dec_pages,
    pre_pos,
    pre_pages,
    w_out,
    moe_gain,
    expert_ids,
    router_logits,
    w_in,
    w_down,
):
    local_rows, width = hidden.shape
    req_count = lax.axis_size("req")
    exp_count = lax.axis_size("exp")
    devices = req_count * exp_count
    group_rows = local_rows * exp_count
    dec_count = dec_len.shape[0]
    segment = group_rows - dec_count
    local_width = w_query.shape[1]
    heads_here = local_width // HD
    page_size = k_pool.shape[1]
    scale = 1.0 / math.sqrt(HD)
    normed_attn = rms_scale(hidden, attn_gain)
    joined = jnp.concatenate([w_query, w_keyval[0], w_keyval[1]], axis=1)
    projected_rows = jnp.dot(
        lax.all_gather(normed_attn, "exp", axis=0, tiled=True),
        joined,
        preferred_element_type=jnp.float32,
    )
    row_index = jnp.arange(group_rows, dtype=jnp.int32)
    dec_index = jnp.minimum(row_index, dec_count - 1)
    positions = jnp.where(
        row_index < dec_count, dec_len[dec_index], pre_pos[0] + row_index - dec_count
    )
    query = rotate(
        projected_rows[:, :local_width].reshape(group_rows, heads_here, HD), positions
    ).astype(jnp.bfloat16)
    keys_new = rotate(
        projected_rows[:, local_width : 2 * local_width].reshape(group_rows, heads_here, HD),
        positions,
    ).astype(jnp.bfloat16)
    values_new = (
        projected_rows[:, 2 * local_width :]
        .reshape(group_rows, heads_here, HD)
        .astype(jnp.bfloat16)
    )
    new_kv = jnp.stack(
        [keys_new.reshape(group_rows, local_width), values_new.reshape(group_rows, local_width)]
    )
    cache_len = dec_pages.shape[1] * page_size
    table_keys = k_pool[dec_pages].reshape(dec_count, cache_len, heads_here, HD)
    table_values = v_pool[dec_pages].reshape(dec_count, cache_len, heads_here, HD)
    dec_query = query[:dec_count]
    dec_scores = (
        jnp.einsum("rhd,rkhd->rhk", dec_query, table_keys, preferred_element_type=jnp.float32)
        * scale
    )
    own_score = (
        jnp.einsum(
            "rhd,rhd->rh", dec_query, keys_new[:dec_count], preferred_element_type=jnp.float32
        )
        * scale
    )
    visible = (jnp.arange(cache_len, dtype=jnp.int32)[None, :] < dec_len[:, None])[:, None, :]
    dec_scores = jnp.where(visible, dec_scores, -jnp.inf)
    highest = jnp.maximum(jnp.max(dec_scores, axis=2), own_score)
    dec_weights = jnp.exp(dec_scores - highest[..., None])
    own_weight = jnp.exp(own_score - highest)
    dec_total = jnp.sum(dec_weights, axis=2) + own_weight
    own_rounded = lax.optimization_barrier(own_weight.astype(jnp.bfloat16)).astype(jnp.float32)
    dec_summed = jnp.einsum(
        "rhk,rkhd->rhd",
        dec_weights.astype(jnp.bfloat16),
        table_values,
        preferred_element_type=jnp.float32,
    )
    dec_summed = dec_summed + own_rounded[..., None] * values_new[:dec_count].astype(jnp.float32)
    dec_out = (
        (dec_summed / dec_total[..., None]).astype(jnp.bfloat16).reshape(dec_count, local_width)
    )
    prefix_count = pre_pages.shape[1]
    block_pages = math.gcd(prefix_count, max(1, 512 // page_size))
    block_keys = block_pages * page_size
    block_count = prefix_count // block_pages
    length = pre_pos[0]
    order = jnp.arange(segment, dtype=jnp.int32)
    causal = order[None, :] <= order[:, None]
    seg_query = query[dec_count:, 0]

    def prefix_step(block, state):
        chosen = lax.dynamic_slice_in_dim(pre_pages[0], block * block_pages, block_pages)
        block_k = k_pool[chosen].reshape(block_keys, HD)
        block_v = v_pool[chosen].reshape(block_keys, HD)
        slots = block * block_keys + jnp.arange(block_keys, dtype=jnp.int32)
        return online_block(state, seg_query, block_k, block_v, (slots < length)[None, :], scale)

    start_state = (
        jnp.full((segment,), -jnp.inf, jnp.float32),
        jnp.zeros((segment,), jnp.float32),
        jnp.zeros((segment, HD), jnp.float32),
    )
    state = lax.fori_loop(0, block_count, prefix_step, start_state)
    state = online_block(
        state, seg_query, keys_new[dec_count:, 0], values_new[dec_count:, 0], causal, scale
    )
    head_outputs = (state[2] / state[1][:, None]).astype(jnp.bfloat16)
    attended = jnp.concatenate([dec_out, head_outputs], axis=0)
    projected = lax.psum_scatter(
        jnp.dot(attended, w_out, preferred_element_type=jnp.float32).astype(jnp.bfloat16),
        "exp",
        scatter_dimension=0,
        tiled=True,
    ).astype(jnp.float32)
    residual = (hidden.astype(jnp.float32) + projected).astype(jnp.bfloat16)
    normed_moe = rms_scale(residual, moe_gain)
    gates = jax.nn.softmax(router_logits, axis=-1)
    if exp_count == 8:
        moe_out = dense_experts(normed_moe, gate_table(expert_ids, gates), w_in, w_down)
    else:
        moe_out = sparse_experts(normed_moe, expert_ids, gates, w_in, w_down)
    mixed = (residual.astype(jnp.float32) + moe_out).astype(jnp.bfloat16)
    return (mixed, new_kv)


def solution(mesh):
    placed = (
        P(("req", "exp"), None),
        P(),
        P(None, "exp"),
        P(None, None, "exp"),
        P("req", None, "exp"),
        P("req", None, "exp"),
        P("req"),
        P("req", None),
        P("req"),
        P("req", None),
        P("exp", None),
        P(),
        P(("req", "exp"), None),
        P(("req", "exp"), None),
        P(("req", "exp"), None, None),
        P(("req", "exp"), None, None),
    )
    return jax.shard_map(
        body,
        mesh=mesh,
        in_specs=placed,
        out_specs=(P(("req", "exp"), None), P(None, "req", "exp")),
        check_vma=False,
    )
```

```python
import functools
import math

import jax
import jax.numpy as jnp
from jax import lax
from jax.experimental import pallas as pl
from jax.experimental.pallas import tpu as pltpu
from jax.sharding import PartitionSpec as P

HD = 128
SPLIT = 2


EPSILON = 1e-05
THETA = 10000.0


WIDE = jnp.float32


def swap(values, bits):
    count = lax.axis_size("exp")
    return lax.ppermute(values, "exp", [(d, d ^ bits) for d in range(count)])


def shift(values, steps):
    count = lax.axis_size("req")
    return lax.ppermute(values, "req", [(d, (d + steps) % count) for d in range(count)])


def plane_gather(rows):
    half = rows.shape[0] // 2
    from_x = swap(rows, 2)
    from_y = swap(rows, 4)
    corner = [swap(from_x[:half], 4), swap(from_y[half:], 2)]
    return [rows, from_x, from_y, jnp.concatenate(corner, axis=0)]


def plane_reduce(parts):
    own, for_x, for_y, corner = parts
    half = own.shape[0] // 2
    via_x = swap(corner[:half], 2)
    via_y = swap(corner[half:], 4)
    sum_y = (for_y[:half].astype(WIDE) + via_x.astype(WIDE)).astype(own.dtype)
    sum_x = (for_x[half:].astype(WIDE) + via_y.astype(WIDE)).astype(own.dtype)
    back_y = swap(jnp.concatenate([sum_y, for_y[half:]], axis=0), 4)
    back_x = swap(jnp.concatenate([for_x[:half], sum_x], axis=0), 2)
    return own.astype(WIDE) + back_x.astype(WIDE) + back_y.astype(WIDE)


def dense_experts(normed_moe, gate_rows, w_in, w_down):
    own_in, own_down = w_in[0], w_down[0]
    pair_in, pair_down = swap(own_in, 1), swap(own_down, 1)
    units = own_down.shape[0]
    req_count = lax.axis_size("req")
    slots = []
    current = normed_moe
    for step in range(req_count):
        slots.append(plane_gather(current))
        if step + 1 < req_count:
            current = shift(current, 1)
    partials = []
    for step in range(req_count):
        rows = jnp.concatenate(slots[step], axis=0)
        total = 0.0
        for part_in, part_down in ((own_in, own_down), (pair_in, pair_down)):
            inner = jnp.dot(rows, part_in, preferred_element_type=WIDE)
            activated = (jax.nn.silu(inner[:, :units]) * inner[:, units:]).astype(jnp.bfloat16)
            total = total + jnp.dot(activated, part_down, preferred_element_type=WIDE)
        scaled = (total * gate_rows[step][:, None]).astype(jnp.bfloat16)
        partials.append(jnp.split(scaled, 4, axis=0))
    result = 0.0
    for step in list(range(1, req_count)) + [0]:
        reduced = plane_reduce(partials[step])
        if step:
            reduced = shift(reduced.astype(jnp.bfloat16), -step).astype(WIDE)
        result = result + reduced
    return result


LOW = -1e30
MIB = 1 << 20


def rope_tables(positions):
    half = HD // 2
    steps = jnp.arange(half, dtype=WIDE)
    frequency = jnp.exp(steps * (-2.0 * math.log(THETA) / HD))
    angles = positions.astype(WIDE)[:, None] * frequency[None, :]
    cosine, sine = jnp.cos(angles), jnp.sin(angles)
    return (
        jnp.concatenate([cosine, cosine], axis=1),
        jnp.concatenate([-sine, sine], axis=1),
    )


def dot_rows(left, right):
    return lax.dot_general(left, right, (((1,), (1,)), ((), ())), preferred_element_type=WIDE)


def attention_kernel(block_count, tile, chunk, *refs):
    place_ref, length_ref, limits_ref, dec_pages_ref, pre_pages_ref = refs[:5]
    blocks = refs[5 : 5 + block_count]
    (weight_ref, same_ref, other_ref, k_pool, v_pool, out_ref, kv_ref) = refs[
        5 + block_count : 12 + block_count
    ]
    (query_s, value_s, pre_k, pre_v, dec_k, dec_v, highest_s, sum_s, pre_sem, dec_sem) = refs[
        12 + block_count :
    ]
    page_size = k_pool.shape[1]
    dec_count, dec_pages = dec_pages_ref.shape
    pre_pages = pre_pages_ref.shape[1]
    rows = query_s.shape[0]
    block_rows = rows // block_count
    dec_keys = dec_pages * page_size
    place = place_ref[0]
    length = length_ref[0]
    rate = math.log2(math.e) / math.sqrt(HD)

    def fetch_prefix(at, carry):
        page = pre_pages_ref[0, at]
        here = pl.ds(pl.multiple_of(at * page_size, page_size), page_size)
        pltpu.make_async_copy(k_pool.at[page], pre_k.at[here], pre_sem.at[0]).start()
        pltpu.make_async_copy(v_pool.at[page], pre_v.at[here, pl.ds(0, HD)], pre_sem.at[1]).start()
        return carry

    lax.fori_loop(0, pre_pages, fetch_prefix, 0)
    for request in range(dec_count):

        def fetch_decode(at, carry):
            page = dec_pages_ref[request, at]
            here = pl.ds(pl.multiple_of(at * page_size, page_size), page_size)
            pltpu.make_async_copy(
                k_pool.at[page], dec_k.at[request, here], dec_sem.at[0, request]
            ).start()
            pltpu.make_async_copy(
                v_pool.at[page], dec_v.at[request, here], dec_sem.at[1, request]
            ).start()
            return carry

        lax.fori_loop(0, dec_pages, fetch_decode, 0)

    ones = jnp.ones((rows, HD), jnp.bfloat16)
    value_s[:, HD:] = ones
    pre_v[:, HD:] = jnp.ones((pre_v.shape[0], HD), jnp.bfloat16)

    for first in range(0, block_count, 2):
        pair = jnp.concatenate([blocks[first][...], blocks[first + 1][...]], axis=0)
        made = jnp.dot(pair, weight_ref[...], preferred_element_type=WIDE)
        for half in range(2):
            mine = made[half * block_rows : (half + 1) * block_rows]
            start = pl.multiple_of((place ^ (first + half)) * block_rows, block_rows)
            here = pl.ds(start, block_rows)
            same, other = same_ref[here, :], other_ref[here, :]
            query, key = mine[:, :HD], mine[:, HD : 2 * HD]
            query_s[here, :] = (query * same + pltpu.roll(query, HD // 2, 1) * other).astype(
                jnp.bfloat16
            )
            kv_ref[0, here, :] = (key * same + pltpu.roll(key, HD // 2, 1) * other).astype(
                jnp.bfloat16
            )
            value = mine[:, 2 * HD :].astype(jnp.bfloat16)
            kv_ref[1, here, :] = value
            value_s[here, :HD] = value

    pltpu.make_async_copy(pre_k, pre_k, pre_sem.at[0]).wait()
    whole_v = pre_v.at[:, pl.ds(0, HD)]
    pltpu.make_async_copy(whole_v, whole_v, pre_sem.at[1]).wait()

    def absorb(scores, values):
        old = highest_s[...]
        new = jnp.maximum(old, jnp.max(scores, axis=1, keepdims=True))
        weights = jnp.exp2(scores - new).astype(jnp.bfloat16)
        sum_s[...] = sum_s[...] * jnp.exp2(old - new) + jnp.dot(
            weights, values, preferred_element_type=WIDE
        )
        highest_s[...] = new

    full = length // chunk

    def one_tile(at, carry):
        start = pl.multiple_of(at * tile, tile)
        query = query_s[pl.ds(start, tile), :]
        highest_s[...] = jnp.full_like(highest_s, LOW)
        sum_s[...] = jnp.zeros_like(sum_s)

        def prefix_chunk(number, masked):
            here = pl.ds(pl.multiple_of(number * chunk, chunk), chunk)
            scores = dot_rows(query, pre_k[here, :]) * rate
            if masked:
                slots = number * chunk + lax.broadcasted_iota(jnp.int32, scores.shape, 1)
                scores = jnp.where(slots < length, scores, LOW)
            absorb(scores, pre_v[here, :])

        def whole_chunk(number, inner):
            prefix_chunk(number, False)
            return inner

        lax.fori_loop(0, full, whole_chunk, 0)

        @pl.when(full * chunk < length)
        def _():
            prefix_chunk(full, True)

        def own_chunk(number, inner):
            here = pl.ds(pl.multiple_of(number * tile, tile), tile)
            scores = dot_rows(query, kv_ref[0, here, :]) * rate
            seen = number * tile + lax.broadcasted_iota(jnp.int32, scores.shape, 1)
            asked = start + lax.broadcasted_iota(jnp.int32, scores.shape, 0)
            allowed = jnp.logical_and(seen >= dec_count, seen <= asked)
            absorb(jnp.where(allowed, scores, LOW), value_s[here, :])
            return inner

        lax.fori_loop(0, at + 1, own_chunk, 0)
        done = (sum_s[:, :HD] / sum_s[:, HD:]).astype(jnp.bfloat16)
        for part in range(tile // block_rows):
            target = (at * (tile // block_rows) + part) ^ place
            target = pl.multiple_of(target * block_rows, block_rows)
            out_ref[pl.ds(target, block_rows), :] = done[
                part * block_rows : (part + 1) * block_rows
            ]
        return carry

    lax.fori_loop(0, rows // tile, one_tile, 0)

    few = 16
    query = query_s[:few, :]
    row = lax.broadcasted_iota(jnp.int32, (few, HD), 0)
    own_scores = dot_rows(query, kv_ref[0, :few, :]) * rate
    first_rows = pl.ds(pl.multiple_of(place * block_rows, block_rows), few)
    result = out_ref[first_rows, :].astype(WIDE)
    for request in range(dec_count):
        pltpu.make_async_copy(dec_k.at[request], dec_k.at[request], dec_sem.at[0, request]).wait()
        pltpu.make_async_copy(dec_v.at[request], dec_v.at[request], dec_sem.at[1, request]).wait()
        scores = dot_rows(query, dec_k[request]) * rate
        slots = lax.broadcasted_iota(jnp.int32, (few, dec_keys), 1)
        scores = jnp.where(slots < limits_ref[request], scores, LOW)
        itself = lax.broadcasted_iota(jnp.int32, (few, few), 1) == request
        own = jnp.where(itself, own_scores, LOW)
        highest = jnp.maximum(
            jnp.max(scores, axis=1, keepdims=True), jnp.max(own, axis=1, keepdims=True)
        )
        weights = jnp.exp2(scores - highest)
        own_weights = jnp.exp2(own - highest)
        total = jnp.sum(weights, axis=1, keepdims=True) + jnp.sum(
            own_weights, axis=1, keepdims=True
        )
        summed = jnp.dot(
            weights.astype(jnp.bfloat16), dec_v[request], preferred_element_type=WIDE
        ) + jnp.dot(
            own_weights.astype(jnp.bfloat16), kv_ref[1, :few, :], preferred_element_type=WIDE
        )
        result = jnp.where(row == request, summed / total, result)
    out_ref[first_rows, :] = result.astype(jnp.bfloat16)


def attention(place, blocks, joined, positions, pools, tables):
    pre_pos, dec_len, dec_pages, pre_pages = tables
    k_pool, v_pool = pools
    rows = sum(block.shape[0] for block in blocks)
    page_size = k_pool.shape[1]
    pre_keys = pre_pages.shape[1] * page_size
    dec_keys = dec_pages.shape[1] * page_size
    dec_count = dec_pages.shape[0]
    tile = 2 * blocks[0].shape[0]
    chunk = math.gcd(pre_keys, 1024)
    same, other = rope_tables(positions)
    number = pl.BlockSpec(memory_space=pltpu.SMEM)
    array = pl.BlockSpec(memory_space=pltpu.VMEM)
    apart = pl.BlockSpec(memory_space=pl.ANY)
    flops = 2 * rows * (joined.size + 2 * HD * (pre_keys + rows))
    return pl.pallas_call(
        functools.partial(attention_kernel, len(blocks), tile, chunk),
        out_shape=(
            jax.ShapeDtypeStruct((rows, HD), jnp.bfloat16),
            jax.ShapeDtypeStruct((2, rows, HD), jnp.bfloat16),
        ),
        in_specs=[number] * 5 + [array] * (len(blocks) + 3) + [apart] * 2,
        out_specs=(array, array),
        scratch_shapes=[
            pltpu.VMEM((rows, HD), jnp.bfloat16),
            pltpu.VMEM((rows, 2 * HD), jnp.bfloat16),
            pltpu.VMEM((pre_keys, HD), jnp.bfloat16),
            pltpu.VMEM((pre_keys, 2 * HD), jnp.bfloat16),
            pltpu.VMEM((dec_count, dec_keys, HD), jnp.bfloat16),
            pltpu.VMEM((dec_count, dec_keys, HD), jnp.bfloat16),
            pltpu.VMEM((tile, 1), WIDE),
            pltpu.VMEM((tile, 2 * HD), WIDE),
            pltpu.SemaphoreType.DMA((2,)),
            pltpu.SemaphoreType.DMA((2, dec_count)),
        ],
        compiler_params=pltpu.CompilerParams(vmem_limit_bytes=44 * MIB),
        cost_estimate=pl.CostEstimate(
            flops=flops, bytes_accessed=20 * MIB, transcendentals=rows * (pre_keys + rows)
        ),
        name="attention",
    )(place, pre_pos, dec_len, dec_pages, pre_pages, *blocks, joined, same, other, k_pool, v_pool)


def project_kernel(count, *refs):
    heads, weights = refs[:count], refs[count : 2 * count]
    hidden_ref, gain_ref, residual_ref, normed_ref, total_s = refs[2 * count :]
    width = hidden_ref.shape[1]
    step = math.gcd(width, 512)
    squares = jnp.zeros((hidden_ref.shape[0], 1), WIDE)
    for start in range(0, width, step):
        here = slice(start, start + step)
        total = hidden_ref[:, here].astype(WIDE)
        for first in range(0, count, 2):
            left = jnp.concatenate([heads[first][...], heads[first + 1][...]], axis=1)
            right = jnp.concatenate(
                [weights[first][:, here], weights[first + 1][:, here]], axis=0
            )
            total = total + jnp.dot(left, right, preferred_element_type=WIDE)
        rounded = total.astype(jnp.bfloat16)
        residual_ref[:, here] = rounded
        total = rounded.astype(WIDE)
        total_s[:, here] = total
        squares = squares + jnp.sum(total * total, axis=1, keepdims=True)
    factor = lax.rsqrt(squares / width + EPSILON)
    normed_ref[...] = (total_s[...] * factor * gain_ref[...]).astype(jnp.bfloat16)


def project(heads, weights, hidden, gain):
    array = pl.BlockSpec(memory_space=pltpu.VMEM)
    count = len(heads)
    return pl.pallas_call(
        functools.partial(project_kernel, count),
        out_shape=(jax.ShapeDtypeStruct(hidden.shape, jnp.bfloat16),) * 2,
        in_specs=[array] * (2 * count + 2),
        out_specs=(array, array),
        scratch_shapes=[pltpu.VMEM(hidden.shape, WIDE)],
        compiler_params=pltpu.CompilerParams(vmem_limit_bytes=32 * MIB),
        cost_estimate=pl.CostEstimate(
            flops=2 * hidden.size * count * HD, bytes_accessed=8 * MIB, transcendentals=0
        ),
        name="project",
    )(*heads, *weights, hidden, gain[None, :])


def norm_kernel(hidden_ref, gain_ref, out_ref):
    values = hidden_ref[...].astype(WIDE)
    factor = lax.rsqrt(jnp.mean(values * values, axis=1, keepdims=True) + EPSILON)
    out_ref[...] = (values * factor * gain_ref[...]).astype(jnp.bfloat16)


def norm(hidden, gain):
    array = pl.BlockSpec(memory_space=pltpu.VMEM)
    return pl.pallas_call(
        norm_kernel,
        out_shape=jax.ShapeDtypeStruct(hidden.shape, jnp.bfloat16),
        in_specs=[array, array],
        out_specs=array,
        compiler_params=pltpu.CompilerParams(vmem_limit_bytes=16 * MIB),
        name="norm",
    )(hidden, gain[None, :])


def gather_blocks(rows):
    near = plane_gather(rows)
    result = []
    for block in near:
        result += [block, swap(block, 1)]
    return result


def gate_table(expert_ids, gates):
    req_count = lax.axis_size("req")
    exp_count = lax.axis_size("exp")
    experts = req_count * exp_count // SPLIT
    named = expert_ids.T[None] == jnp.arange(experts, dtype=jnp.int32)[:, None, None]
    table = jnp.sum(jnp.where(named, gates.T[None], 0.0), axis=1)
    near = jnp.stack([table] + [shift(table, step) for step in range(1, req_count)])
    around = [near] + [swap(near, bits) for bits in range(2, exp_count, 2)]
    mine = (lax.axis_index("req") * exp_count + lax.axis_index("exp")) // SPLIT
    chosen = jnp.arange(experts) == mine
    column = [jnp.sum(jnp.where(chosen[:, None], part, 0.0), axis=1) for part in around]
    return jnp.stack(column, axis=1).reshape(req_count, -1)


def deliver(buffer):
    result = lax.all_to_all(buffer, ("req", "exp"), split_axis=0, concat_axis=0, tiled=True)
    return result


def bring_back(buffer):
    result = lax.all_to_all(buffer, ("req", "exp"), split_axis=0, concat_axis=0, tiled=True)
    return result


def sparse_experts(normed_moe, expert_ids, gates, w_in, w_down):
    local_rows, width = normed_moe.shape
    devices = lax.axis_size("req") * lax.axis_size("exp")
    experts = devices // SPLIT
    top = expert_ids.shape[1]
    capacity = 2 * ((local_rows * top * 5 + 8 * experts - 1) // (8 * experts))
    assigned = expert_ids.reshape(-1)
    count_all = assigned.shape[0]
    marks = (assigned[:, None] == jnp.arange(experts, dtype=jnp.int32)[None, :]).astype(jnp.int32)
    earlier = jnp.cumsum(marks, axis=0) - marks
    place = jnp.sum(earlier * marks, axis=1)
    target = assigned * capacity + place
    owner_rows = jnp.arange(count_all, dtype=jnp.int32) // top
    outgoing = (
        jnp.zeros((experts * capacity, width), jnp.bfloat16).at[target].set(normed_moe[owner_rows])
    )
    doubled = jnp.broadcast_to(
        outgoing.reshape(experts, 1, capacity, width), (experts, SPLIT, capacity, width)
    ).reshape(devices, capacity, width)
    arrived = deliver(doubled)
    piece_units = w_down.shape[1]
    inner = jnp.dot(
        arrived.reshape(devices * capacity, width), w_in[0], preferred_element_type=jnp.float32
    )
    activated = (jax.nn.silu(inner[:, :piece_units]) * inner[:, piece_units:]).astype(jnp.bfloat16)
    partial_value = (
        jnp.dot(activated, w_down[0], preferred_element_type=jnp.float32)
        .astype(jnp.bfloat16)
        .reshape(devices, capacity, width)
    )
    returned = bring_back(partial_value).reshape(devices * capacity, width)
    base_index = assigned * (SPLIT * capacity) + place
    lower_half = returned[base_index].astype(jnp.float32)
    upper_half = returned[base_index + capacity].astype(jnp.float32)
    weighted = (lower_half + upper_half) * gates.reshape(-1)[:, None]
    moe_out = jnp.sum(weighted.reshape(local_rows, top, width), axis=1)
    return moe_out


def body(
    hidden,
    attn_gain,
    w_query,
    w_keyval,
    k_pool,
    v_pool,
    dec_len,
    dec_pages,
    pre_pos,
    pre_pages,
    w_out,
    moe_gain,
    expert_ids,
    router_logits,
    w_in,
    w_down,
):
    local_rows, width = hidden.shape
    exp_count = lax.axis_size("exp")
    group_rows = local_rows * exp_count
    dec_count = dec_len.shape[0]
    quick = exp_count == 8
    normed_attn = norm(hidden, attn_gain)
    joined = jnp.concatenate([w_query, w_keyval[0], w_keyval[1]], axis=1)
    row_index = jnp.arange(group_rows, dtype=jnp.int32)
    own_positions = jnp.sum(
        jnp.where(row_index[:, None] == jnp.arange(dec_count), dec_len[None, :], 0), axis=1
    )
    positions = jnp.where(row_index < dec_count, own_positions, pre_pos[0] + row_index - dec_count)
    if quick:
        place = lax.axis_index("exp").reshape(1)
        blocks = gather_blocks(normed_attn)
        out_blocks = gather_blocks(w_out)
    else:
        place = jnp.zeros((1,), jnp.int32)
        blocks = jnp.split(lax.all_gather(normed_attn, "exp", axis=0, tiled=True), exp_count)
        out_blocks = jnp.split(lax.all_gather(w_out, "exp", axis=0, tiled=True), exp_count)
    attended, new_kv = attention(
        place,
        blocks,
        joined,
        positions,
        (k_pool, v_pool),
        (pre_pos, dec_len, dec_pages, pre_pages),
    )
    if quick:
        mine = jnp.split(attended, exp_count)
        heads = [mine[0]] + [swap(mine[bits], bits) for bits in range(1, exp_count)]
    else:
        heads = jnp.split(
            lax.all_to_all(attended, "exp", split_axis=0, concat_axis=0, tiled=True), exp_count
        )
    residual, normed_moe = project(heads, out_blocks, hidden, moe_gain)
    gates = jax.nn.softmax(router_logits, axis=-1)
    if quick:
        moe_out = dense_experts(normed_moe, gate_table(expert_ids, gates), w_in, w_down)
    else:
        moe_out = sparse_experts(normed_moe, expert_ids, gates, w_in, w_down)
    mixed = (residual.astype(jnp.float32) + moe_out).astype(jnp.bfloat16)
    return (mixed, new_kv)


def solution(mesh):
    placed = (
        P(("req", "exp"), None),
        P(),
        P(None, "exp"),
        P(None, None, "exp"),
        P("req", None, "exp"),
        P("req", None, "exp"),
        P("req"),
        P("req", None),
        P("req"),
        P("req", None),
        P("exp", None),
        P(),
        P(("req", "exp"), None),
        P(("req", "exp"), None),
        P(("req", "exp"), None, None),
        P(("req", "exp"), None, None),
    )
    return jax.shard_map(
        body,
        mesh=mesh,
        in_specs=placed,
        out_specs=(P(("req", "exp"), None), P(None, "req", "exp")),
        check_vma=False,
    )
```

```python
import functools
import math

import jax
import jax.numpy as jnp
from jax import lax
from jax.experimental import pallas as pl
from jax.experimental.pallas import tpu as pltpu
from jax.sharding import PartitionSpec as P

HD = 128
SPLIT = 2


EPSILON = 1e-05
THETA = 10000.0


WIDE = jnp.float32


def swap(values, bits):
    count = lax.axis_size("exp")
    return lax.ppermute(values, "exp", [(d, d ^ bits) for d in range(count)])


def shift(values, steps):
    count = lax.axis_size("req")
    return lax.ppermute(values, "req", [(d, (d + steps) % count) for d in range(count)])


def after(values, *others):
    return lax.optimization_barrier((values, *others))[0]


def experts_kernel(part, wide, *refs):
    blocks, (own_in, own_down, pair_in, pair_down) = refs[:4], refs[4:8]
    outs = refs[8:12]
    rows_s, in_s, down_s, active_s, made_s, block_sem, in_sem, down_sem, out_sem = refs[12:]
    units, width = own_down.shape
    size = blocks[0].shape[0]
    parts, tiles = units // part, width // wide

    loads = [
        pltpu.make_async_copy(block, rows_s.at[pl.ds(at * size, size)], block_sem.at[at])
        for at, block in enumerate(blocks)
    ]
    arrivals = []
    for piece, weight in enumerate((own_in, pair_in)):
        for at in range(parts):
            number = piece * parts + at
            here = pl.ds(number * 2 * part, part), pl.ds((number * 2 + 1) * part, part)
            arrivals.append(
                [
                    pltpu.make_async_copy(
                        weight.at[:, pl.ds(half * units + at * part, part)],
                        in_s.at[:, here[half]],
                        in_sem.at[2 * number + half],
                    )
                    for half in range(2)
                ]
            )
    downs = [
        pltpu.make_async_copy(weight, down_s.at[pl.ds(piece * units, units)], down_sem.at[piece])
        for piece, weight in enumerate((own_down, pair_down))
    ]
    for copy in loads:
        copy.start()
    for pair in arrivals:
        for copy in pair:
            copy.start()
    for copy in downs:
        copy.start()
    for copy in loads:
        copy.wait()
    rows = rows_s[...]
    for number, pair in enumerate(arrivals):
        for copy in pair:
            copy.wait()
        both = jnp.dot(
            rows,
            in_s[:, 2 * part * number : 2 * part * (number + 1)],
            preferred_element_type=WIDE,
        )
        gate, up = both[:, :part], both[:, part:]
        active = gate / (1.0 + jnp.exp(-gate)) * up
        active_s[:, part * number : part * (number + 1)] = active.astype(jnp.bfloat16)
    for copy in downs:
        copy.wait()
    active = active_s[...]
    stores = []
    for tile in range(tiles):
        here = slice(tile * wide, (tile + 1) * wide)
        made = jnp.dot(active, down_s[:, here], preferred_element_type=WIDE)
        for at, out in enumerate(outs):
            mine = slice(at * size, (at + 1) * size)
            made_s[mine, here] = made[mine].astype(jnp.bfloat16)
            copy = pltpu.make_async_copy(
                made_s.at[pl.ds(at * size, size), pl.ds(tile * wide, wide)],
                out.at[:, pl.ds(tile * wide, wide)],
                out_sem.at[tile * len(outs) + at],
            )
            copy.start()
            stores.append(copy)
    for copy in stores:
        copy.wait()


def expert_rows(blocks, pieces):
    (own_in, own_down), (pair_in, pair_down) = pieces
    units, width = own_down.shape
    size, count = blocks[0].shape[0], len(blocks)
    rows = size * count
    part, wide = math.gcd(units, 256), math.gcd(width, 512)
    apart = pl.BlockSpec(memory_space=pl.ANY)
    return pl.pallas_call(
        functools.partial(experts_kernel, part, wide),
        out_shape=[jax.ShapeDtypeStruct((size, width), jnp.bfloat16)] * count,
        in_specs=[apart] * (count + 4),
        out_specs=[apart] * count,
        scratch_shapes=[
            pltpu.VMEM((rows, width), jnp.bfloat16),
            pltpu.VMEM((width, 4 * units), jnp.bfloat16),
            pltpu.VMEM((2 * units, width), jnp.bfloat16),
            pltpu.VMEM((rows, 2 * units), jnp.bfloat16),
            pltpu.VMEM((rows, width), jnp.bfloat16),
            pltpu.SemaphoreType.DMA((count,)),
            pltpu.SemaphoreType.DMA((4 * (units // part),)),
            pltpu.SemaphoreType.DMA((2,)),
            pltpu.SemaphoreType.DMA((count * (width // wide),)),
        ],
        compiler_params=pltpu.CompilerParams(vmem_limit_bytes=30 * MIB),
        cost_estimate=pl.CostEstimate(
            flops=12 * rows * width * units,
            bytes_accessed=16 * MIB,
            transcendentals=2 * rows * units,
        ),
        name="experts",
    )(*blocks, own_in, own_down, pair_in, pair_down)


def pick_kernel(gate_ref, place_ref, rows_ref, *refs):
    outs, (made_s, sem) = refs[:-2], refs[-2:]
    rows = rows_ref[...]
    capacity = outs[0].shape[0]
    stores = []
    for at, out in enumerate(outs):
        room = lax.broadcasted_iota(jnp.int32, (capacity, rows.shape[0]), 0)
        chosen = jnp.logical_and(gate_ref[at : at + 1, :] > 0, place_ref[at : at + 1, :] == room)
        picked = jnp.where(chosen, 1.0, 0.0).astype(jnp.bfloat16)
        made = jnp.dot(picked, rows, preferred_element_type=WIDE).astype(jnp.bfloat16)
        made_s[at * capacity : (at + 1) * capacity, :] = made
        copy = pltpu.make_async_copy(
            made_s.at[pl.ds(at * capacity, capacity)], out, sem.at[at]
        )
        copy.start()
        stores.append(copy)
    for copy in stores:
        copy.wait()


def pick(rows, gates, places, count, capacity):
    array = pl.BlockSpec(memory_space=pltpu.VMEM)
    width = rows.shape[1]
    return pl.pallas_call(
        pick_kernel,
        out_shape=[jax.ShapeDtypeStruct((capacity, width), jnp.bfloat16)] * count,
        in_specs=[array] * 3,
        out_specs=[pl.BlockSpec(memory_space=pl.ANY)] * count,
        scratch_shapes=[
            pltpu.VMEM((count * capacity, width), jnp.bfloat16),
            pltpu.SemaphoreType.DMA((count,)),
        ],
        compiler_params=pltpu.CompilerParams(vmem_limit_bytes=12 * MIB),
        cost_estimate=pl.CostEstimate(
            flops=2 * count * capacity * rows.size, bytes_accessed=MIB, transcendentals=0
        ),
        name="pick",
    )(gates, places, rows)


def merge_kernel(count, gate_ref, place_ref, *refs):
    parts, terms, (out_ref, parts_s, sem) = refs[:count], refs[count:-3], refs[-3:]
    capacity = parts[0].shape[0]
    loads = []
    for at, part in enumerate(parts):
        here = parts_s.at[pl.ds(at * capacity, capacity)]
        loads.append(pltpu.make_async_copy(part, here, sem.at[at]))
        loads[-1].start()
    gates, places = gate_ref[...].T, place_ref[...].T
    total = 0.0
    for at in range(count):
        gate, place = gates[:, at : at + 1], places[:, at : at + 1]
        room = lax.broadcasted_iota(jnp.int32, (gates.shape[0], capacity), 1)
        chosen = jnp.logical_and(gate > 0, place == room)
        spread = jnp.where(chosen, 1.0, 0.0).astype(jnp.bfloat16)
        loads[at].wait()
        part = parts_s[at * capacity : (at + 1) * capacity, :]
        total = total + gate * jnp.dot(spread, part, preferred_element_type=WIDE)
    for term in terms:
        total = total + term[...].astype(WIDE)
    out_ref[...] = total.astype(jnp.bfloat16)


def merge(parts, gates, places, terms):
    array = pl.BlockSpec(memory_space=pltpu.VMEM)
    count, (capacity, width) = len(parts), parts[0].shape
    rows = gates.shape[1]
    return pl.pallas_call(
        functools.partial(merge_kernel, count),
        out_shape=jax.ShapeDtypeStruct((rows, width), jnp.bfloat16),
        in_specs=[array] * 2
        + [pl.BlockSpec(memory_space=pl.ANY)] * count
        + [array] * len(terms),
        out_specs=array,
        scratch_shapes=[
            pltpu.VMEM((count * capacity, width), jnp.bfloat16),
            pltpu.SemaphoreType.DMA((count,)),
        ],
        compiler_params=pltpu.CompilerParams(vmem_limit_bytes=16 * MIB),
        cost_estimate=pl.CostEstimate(
            flops=2 * rows * width * count * capacity, bytes_accessed=MIB, transcendentals=0
        ),
        name="merge",
    )(gates, places, *parts, *terms)


def plane_experts(normed_moe, residual, gates, places, pieces, capacity):
    steps = lax.axis_size("req")
    count = lax.axis_size("exp") // 2
    rounds = []

    def exchange(parts):
        mine, *others = parts
        others = after(tuple(others), *rounds[-2:-1])
        rounds.append(tuple(swap(part, 2 * at) for at, part in enumerate(others, 1)))
        return [mine, *rounds[-1]]

    moved, came = normed_moe, []
    for step in range(steps):
        following = shift(moved, 1) if step + 1 < steps else None
        came.append(exchange(pick(moved, gates[step], places[step], count, capacity)))
        moved = following if step else after(following, rounds[0])
    made = []
    for step in range(steps):
        made.append(expert_rows(after(came[step], *made[-1:]), pieces))
    sums = []
    for step in range(1, steps):
        sums.append(merge(exchange(made[step]), gates[step], places[step], []))
    terms = [shift(total, -step) for step, total in enumerate(sums, 1)]
    return merge(exchange(made[0]), gates[0], places[0], [*terms, residual])


LOW = -1e30
MIB = 1 << 20


def rope_tables(positions):
    half = HD // 2
    steps = jnp.arange(half, dtype=WIDE)
    frequency = jnp.exp(steps * (-2.0 * math.log(THETA) / HD))
    angles = positions.astype(WIDE)[:, None] * frequency[None, :]
    cosine, sine = jnp.cos(angles), jnp.sin(angles)
    return (
        jnp.concatenate([cosine, cosine], axis=1),
        jnp.concatenate([-sine, sine], axis=1),
    )


def dot_rows(left, right):
    return lax.dot_general(left, right, (((1,), (1,)), ((), ())), preferred_element_type=WIDE)


def attention_kernel(layout, block_rows, tile, *refs):
    ref_count = sum(count for count, _ in layout)
    place_ref, length_ref, limits_ref, dec_pages_ref, pre_pages_ref = refs[:5]
    sources = refs[5 : 5 + ref_count]
    w_query, w_keyval, same_ref, other_ref, k_pool, v_pool, _, out_ref, kv_ref = refs[
        5 + ref_count : 14 + ref_count
    ]
    (rows_s, weight_s, query_s, turned_s, pre_k, pre_v, dec_k, dec_v) = refs[
        14 + ref_count : 22 + ref_count
    ]
    row_sem, weight_sem, pre_sem, dec_sem = refs[22 + ref_count :]
    page_size = k_pool.shape[1]
    dec_count, dec_pages = dec_pages_ref.shape
    pre_pages = pre_pages_ref.shape[1]
    pre_keys = pre_pages * page_size
    rows = query_s.shape[0]
    dec_keys = dec_pages * page_size
    place = place_ref[0]
    length = length_ref[0]
    rate = math.log2(math.e) / math.sqrt(HD)

    weight_copies = [
        pltpu.make_async_copy(part, weight_s.at[:, pl.ds(at * HD, HD)], weight_sem.at[at])
        for at, part in enumerate((w_query, w_keyval.at[0], w_keyval.at[1]))
    ]
    row_copies, start = [], 0
    for at, source in enumerate(sources):
        here = rows_s.at[pl.ds(start, source.shape[0])]
        row_copies.append(pltpu.make_async_copy(source, here, row_sem.at[at]))
        start += source.shape[0]
    for copy in weight_copies + row_copies:
        copy.start()

    def fetch_prefix(at, carry):
        page = pre_pages_ref[0, at]
        here = pl.ds(pl.multiple_of(at * page_size, page_size), page_size)
        pltpu.make_async_copy(k_pool.at[page], pre_k.at[here], pre_sem.at[0]).start()
        pltpu.make_async_copy(v_pool.at[page], pre_v.at[here], pre_sem.at[1]).start()
        return carry

    lax.fori_loop(0, pre_pages, fetch_prefix, 0)
    for request in range(dec_count):

        def fetch_decode(at, carry):
            page = dec_pages_ref[request, at]
            here = pl.ds(pl.multiple_of(at * page_size, page_size), page_size)
            pltpu.make_async_copy(
                k_pool.at[page], dec_k.at[request, here], dec_sem.at[0, request]
            ).start()
            pltpu.make_async_copy(
                v_pool.at[page], dec_v.at[request, here], dec_sem.at[1, request]
            ).start()
            return carry

        lax.fori_loop(0, dec_pages, fetch_decode, 0)

    for copy in weight_copies:
        copy.wait()
    start = 0
    for count, names in layout:
        for _ in range(count):
            row_copies.pop(0).wait()
        size = block_rows * len(names)
        made = jnp.dot(rows_s[start : start + size], weight_s[...], preferred_element_type=WIDE)
        start += size
        for at, name in enumerate(names):
            mine = made[at * block_rows : (at + 1) * block_rows]
            first = pl.multiple_of((place ^ name) * block_rows, block_rows)
            here = pl.ds(first, block_rows)
            same, other = same_ref[here, :], other_ref[here, :]
            query, key = mine[:, :HD], mine[:, HD : 2 * HD]
            query_s[here, :] = (query * same + pltpu.roll(query, HD // 2, 1) * other).astype(
                jnp.bfloat16
            )
            kv_ref[0, here, :] = (key * same + pltpu.roll(key, HD // 2, 1) * other).astype(
                jnp.bfloat16
            )
            kv_ref[1, here, :] = mine[:, 2 * HD :].astype(jnp.bfloat16)

    pltpu.make_async_copy(pre_k, pre_k, pre_sem.at[0]).wait()
    pltpu.make_async_copy(pre_v, pre_v, pre_sem.at[1]).wait()

    turned_s[:HD, :pre_keys] = pre_v[...].T
    turned_s[:HD, pre_keys:] = kv_ref[1].T
    turned_s[HD:, :] = jnp.ones((turned_s.shape[0] - HD, turned_s.shape[1]), jnp.bfloat16)
    slots = lax.broadcasted_iota(jnp.int32, (pre_keys, 1), 0)
    bias = jnp.where(slots < length, 0.0, LOW)
    for at in range(rows // tile):
        start = at * tile
        held = start + tile
        query = query_s[start:held, :]
        scores = dot_rows(pre_k[...], query) * rate + bias
        own = dot_rows(kv_ref[0, :held, :], query) * rate
        seen = lax.broadcasted_iota(jnp.int32, own.shape, 0)
        asked = start + lax.broadcasted_iota(jnp.int32, own.shape, 1)
        own = jnp.where(jnp.logical_and(seen >= dec_count, seen <= asked), own, LOW)
        highest = jnp.maximum(
            jnp.max(scores, axis=0, keepdims=True), jnp.max(own, axis=0, keepdims=True)
        )
        weights = jnp.exp2(scores - highest).astype(jnp.bfloat16)
        own_weights = jnp.exp2(own - highest).astype(jnp.bfloat16)
        total = jnp.dot(
            turned_s[:, :pre_keys], weights, preferred_element_type=WIDE
        ) + jnp.dot(
            turned_s[:, pre_keys : pre_keys + held], own_weights, preferred_element_type=WIDE
        )
        done = (total[:HD] / total[HD : HD + 1]).T.astype(jnp.bfloat16)
        for part in range(tile // block_rows):
            target = (at * (tile // block_rows) + part) ^ place
            target = pl.multiple_of(target * block_rows, block_rows)
            out_ref[pl.ds(target, block_rows), :] = done[
                part * block_rows : (part + 1) * block_rows
            ]

    few = 16
    query = query_s[:few, :]
    row = lax.broadcasted_iota(jnp.int32, (few, HD), 0)
    own_scores = dot_rows(query, kv_ref[0, :few, :]) * rate
    first_rows = pl.ds(pl.multiple_of(place * block_rows, block_rows), few)
    result = out_ref[first_rows, :].astype(WIDE)
    for request in range(dec_count):
        pltpu.make_async_copy(dec_k.at[request], dec_k.at[request], dec_sem.at[0, request]).wait()
        pltpu.make_async_copy(dec_v.at[request], dec_v.at[request], dec_sem.at[1, request]).wait()
        scores = dot_rows(query, dec_k[request]) * rate
        slots = lax.broadcasted_iota(jnp.int32, (few, dec_keys), 1)
        scores = jnp.where(slots < limits_ref[request], scores, LOW)
        itself = lax.broadcasted_iota(jnp.int32, (few, few), 1) == request
        own = jnp.where(itself, own_scores, LOW)
        highest = jnp.maximum(
            jnp.max(scores, axis=1, keepdims=True), jnp.max(own, axis=1, keepdims=True)
        )
        weights = jnp.exp2(scores - highest)
        own_weights = jnp.exp2(own - highest)
        total = jnp.sum(weights, axis=1, keepdims=True) + jnp.sum(
            own_weights, axis=1, keepdims=True
        )
        summed = jnp.dot(
            weights.astype(jnp.bfloat16), dec_v[request], preferred_element_type=WIDE
        ) + jnp.dot(
            own_weights.astype(jnp.bfloat16), kv_ref[1, :few, :], preferred_element_type=WIDE
        )
        result = jnp.where(row == request, summed / total, result)
    out_ref[first_rows, :] = result.astype(jnp.bfloat16)


def attention(place, groups, names, weights, positions, pools, tables, earlier):
    pre_pos, dec_len, dec_pages, pre_pages = tables
    k_pool, v_pool = pools
    w_query, w_keyval = weights
    blocks = [block for group in groups for block in group]
    rows = sum(block.shape[0] for block in blocks)
    block_rows = rows // sum(len(group) for group in names)
    layout = [(len(group), name) for group, name in zip(groups, names, strict=True)]
    page_size = k_pool.shape[1]
    pre_keys = pre_pages.shape[1] * page_size
    dec_keys = dec_pages.shape[1] * page_size
    dec_count = dec_pages.shape[0]
    tile = 4 * block_rows
    width = w_query.shape[0]
    same, other = rope_tables(positions)
    number = pl.BlockSpec(memory_space=pltpu.SMEM)
    array = pl.BlockSpec(memory_space=pltpu.VMEM)
    apart = pl.BlockSpec(memory_space=pl.ANY)
    flops = 2 * rows * (3 * HD * width + 2 * HD * (pre_keys + rows))
    return pl.pallas_call(
        functools.partial(attention_kernel, layout, block_rows, tile),
        out_shape=(
            jax.ShapeDtypeStruct((rows, HD), jnp.bfloat16),
            jax.ShapeDtypeStruct((2, rows, HD), jnp.bfloat16),
        ),
        in_specs=[number] * 5 + [apart] * (len(blocks) + 2) + [array] * 2 + [apart] * 3,
        out_specs=(array, array),
        scratch_shapes=[
            pltpu.VMEM((rows, width), jnp.bfloat16),
            pltpu.VMEM((width, 3 * HD), jnp.bfloat16),
            pltpu.VMEM((rows, HD), jnp.bfloat16),
            pltpu.VMEM((HD + 16, pre_keys + rows), jnp.bfloat16),
            pltpu.VMEM((pre_keys, HD), jnp.bfloat16),
            pltpu.VMEM((pre_keys, HD), jnp.bfloat16),
            pltpu.VMEM((dec_count, dec_keys, HD), jnp.bfloat16),
            pltpu.VMEM((dec_count, dec_keys, HD), jnp.bfloat16),
            pltpu.SemaphoreType.DMA((len(blocks),)),
            pltpu.SemaphoreType.DMA((3,)),
            pltpu.SemaphoreType.DMA((2,)),
            pltpu.SemaphoreType.DMA((2, dec_count)),
        ],
        compiler_params=pltpu.CompilerParams(vmem_limit_bytes=48 * MIB),
        cost_estimate=pl.CostEstimate(
            flops=flops, bytes_accessed=20 * MIB, transcendentals=rows * (pre_keys + rows)
        ),
        name="attention",
    )(
        place,
        pre_pos,
        dec_len,
        dec_pages,
        pre_pages,
        *blocks,
        w_query,
        w_keyval,
        same,
        other,
        k_pool,
        v_pool,
        earlier,
    )


def project_kernel(count, *refs):
    heads, weights = refs[:count], refs[count : 2 * count]
    own_ref, other_ref = refs[2 * count :]
    width = weights[0].shape[1]
    rows = own_ref.shape[0]
    step = math.gcd(width, 512)
    for start in range(0, width, step):
        here = slice(start, start + step)
        total = 0.0
        for first in range(0, count, 2):
            left = jnp.concatenate([heads[first][...], heads[first + 1][...]], axis=1)
            right = jnp.concatenate(
                [weights[first][:, here], weights[first + 1][:, here]], axis=0
            )
            total = total + jnp.dot(left, right, preferred_element_type=WIDE)
        own_ref[:, here] = total[:rows]
        other_ref[:, here] = total[rows:].astype(jnp.bfloat16)


def project(heads, weights, rows):
    array = pl.BlockSpec(memory_space=pltpu.VMEM)
    count, all_rows, width = len(heads), heads[0].shape[0], weights[0].shape[1]
    return pl.pallas_call(
        functools.partial(project_kernel, count),
        out_shape=(
            jax.ShapeDtypeStruct((rows, width), WIDE),
            jax.ShapeDtypeStruct((all_rows - rows, width), jnp.bfloat16),
        ),
        in_specs=[array] * (2 * count),
        out_specs=(array, array),
        compiler_params=pltpu.CompilerParams(vmem_limit_bytes=32 * MIB),
        cost_estimate=pl.CostEstimate(
            flops=2 * all_rows * width * count * HD, bytes_accessed=4 * MIB, transcendentals=0
        ),
        name="project",
    )(*heads, *weights)


def close_kernel(hidden_ref, gain_ref, *refs):
    *terms, residual_ref, normed_ref = refs
    total = hidden_ref[...].astype(WIDE)
    for term in terms:
        total = total + term[...].astype(WIDE)
    rounded = total.astype(jnp.bfloat16)
    residual_ref[...] = rounded
    total = rounded.astype(WIDE)
    factor = lax.rsqrt(jnp.mean(total * total, axis=1, keepdims=True) + EPSILON)
    normed_ref[...] = (total * factor * gain_ref[...]).astype(jnp.bfloat16)


def close(hidden, gain, terms):
    array = pl.BlockSpec(memory_space=pltpu.VMEM)
    return pl.pallas_call(
        close_kernel,
        out_shape=(jax.ShapeDtypeStruct(hidden.shape, jnp.bfloat16),) * 2,
        in_specs=[array] * (2 + len(terms)),
        out_specs=(array, array),
        compiler_params=pltpu.CompilerParams(vmem_limit_bytes=16 * MIB),
        name="close",
    )(hidden, gain[None, :], *terms)


def norm_kernel(hidden_ref, gain_ref, out_ref):
    values = hidden_ref[...].astype(WIDE)
    factor = lax.rsqrt(jnp.mean(values * values, axis=1, keepdims=True) + EPSILON)
    out_ref[...] = (values * factor * gain_ref[...]).astype(jnp.bfloat16)


def norm(hidden, gain):
    array = pl.BlockSpec(memory_space=pltpu.VMEM)
    return pl.pallas_call(
        norm_kernel,
        out_shape=jax.ShapeDtypeStruct(hidden.shape, jnp.bfloat16),
        in_specs=[array, array],
        out_specs=array,
        compiler_params=pltpu.CompilerParams(vmem_limit_bytes=16 * MIB),
        name="norm",
    )(hidden, gain[None, :])


def gather_blocks(rows, first):
    half = rows.shape[0] // 2
    from_x, from_y = swap(rows, 2), swap(rows, 4)
    beside = swap(after(rows, from_x), 1)
    x_1, y_2 = after((from_x[:half], from_y[half:]), *first)
    far = jnp.concatenate([swap(x_1, 4), swap(y_2, 2)], axis=0)
    near = jnp.concatenate([from_x, from_y], axis=0)
    near_beside = swap(near, 1)
    return (
        [[rows, beside], [near], [near_beside], [far, swap(far, 1)]],
        [[0, 1], [2, 4], [3, 5], [6, 7]],
    )


def gate_table(expert_ids, gates):
    req_count = lax.axis_size("req")
    exp_count = lax.axis_size("exp")
    experts = req_count * exp_count // SPLIT
    named = expert_ids.T[None] == jnp.arange(experts, dtype=jnp.int32)[:, None, None]
    table = jnp.sum(jnp.where(named, gates.T[None], 0.0), axis=1)
    near = jnp.stack([table, shift(table, 1)])
    near = jnp.concatenate([near, shift(near, 2)])
    bits = jnp.arange(0, exp_count, 2, dtype=jnp.int32)
    owner = lax.axis_index("req") * exp_count + (lax.axis_index("exp") ^ bits)
    chosen = (owner // SPLIT)[:, None] == jnp.arange(experts, dtype=jnp.int32)
    mine = jnp.sum(jnp.where(chosen[None, :, :, None], near[:, None], 0.0), axis=2)
    mine = jnp.pad(mine, ((0, 0), (0, -mine.shape[1] % 8), (0, 0)))
    marks = (mine > 0).astype(jnp.int32)
    return mine, jnp.cumsum(marks, axis=2) - marks


def deliver(buffer):
    result = lax.all_to_all(buffer, ("req", "exp"), split_axis=0, concat_axis=0, tiled=True)
    return result


def bring_back(buffer):
    result = lax.all_to_all(buffer, ("req", "exp"), split_axis=0, concat_axis=0, tiled=True)
    return result


def slots_of(choices, experts):
    return 2 * ((choices * 5 + 8 * experts - 1) // (8 * experts))


def sparse_experts(normed_moe, expert_ids, gates, w_in, w_down):
    local_rows, width = normed_moe.shape
    devices = lax.axis_size("req") * lax.axis_size("exp")
    experts = devices // SPLIT
    top = expert_ids.shape[1]
    capacity = slots_of(local_rows * top, experts)
    assigned = expert_ids.reshape(-1)
    count_all = assigned.shape[0]
    marks = (assigned[:, None] == jnp.arange(experts, dtype=jnp.int32)[None, :]).astype(jnp.int32)
    earlier = jnp.cumsum(marks, axis=0) - marks
    place = jnp.sum(earlier * marks, axis=1)
    target = assigned * capacity + place
    owner_rows = jnp.arange(count_all, dtype=jnp.int32) // top
    outgoing = (
        jnp.zeros((experts * capacity, width), jnp.bfloat16).at[target].set(normed_moe[owner_rows])
    )
    doubled = jnp.broadcast_to(
        outgoing.reshape(experts, 1, capacity, width), (experts, SPLIT, capacity, width)
    ).reshape(devices, capacity, width)
    arrived = deliver(doubled)
    piece_units = w_down.shape[1]
    inner = jnp.dot(
        arrived.reshape(devices * capacity, width), w_in[0], preferred_element_type=jnp.float32
    )
    activated = (jax.nn.silu(inner[:, :piece_units]) * inner[:, piece_units:]).astype(jnp.bfloat16)
    partial_value = (
        jnp.dot(activated, w_down[0], preferred_element_type=jnp.float32)
        .astype(jnp.bfloat16)
        .reshape(devices, capacity, width)
    )
    returned = bring_back(partial_value).reshape(devices * capacity, width)
    base_index = assigned * (SPLIT * capacity) + place
    lower_half = returned[base_index].astype(jnp.float32)
    upper_half = returned[base_index + capacity].astype(jnp.float32)
    weighted = (lower_half + upper_half) * gates.reshape(-1)[:, None]
    moe_out = jnp.sum(weighted.reshape(local_rows, top, width), axis=1)
    return moe_out


def body(
    hidden,
    attn_gain,
    w_query,
    w_keyval,
    k_pool,
    v_pool,
    dec_len,
    dec_pages,
    pre_pos,
    pre_pages,
    w_out,
    moe_gain,
    expert_ids,
    router_logits,
    w_in,
    w_down,
):
    local_rows, width = hidden.shape
    exp_count = lax.axis_size("exp")
    group_rows = local_rows * exp_count
    dec_count = dec_len.shape[0]
    quick = exp_count == 8
    experts = lax.axis_size("req") * exp_count // SPLIT
    capacity = slots_of(local_rows * expert_ids.shape[1], experts)
    normed_attn = norm(hidden, attn_gain)
    row_index = jnp.arange(group_rows, dtype=jnp.int32)
    own_positions = jnp.sum(
        jnp.where(row_index[:, None] == jnp.arange(dec_count), dec_len[None, :], 0), axis=1
    )
    positions = jnp.where(row_index < dec_count, own_positions, pre_pos[0] + row_index - dec_count)
    if quick:
        place = lax.axis_index("exp").reshape(1)
        gates = jax.nn.softmax(router_logits, axis=-1)
        near_gates, near_places = gate_table(expert_ids, gates)
        own_in, own_down = w_in[0], w_down[0]
        pair_in = swap(own_in, 1)
        groups, names = gather_blocks(normed_attn, (near_places, pair_in))
        far, late = groups[-1]
        own_out, late_down = after(w_out, far), after(own_down, late)
        out_blocks = [w_out] + [swap(own_out, bits) for bits in (2, 4, 6)]
        pieces = [(own_in, own_down), (pair_in, swap(late_down, 1))]
        earlier = near_places
    else:
        place = jnp.zeros((1,), jnp.int32)
        earlier = place
        blocks = jnp.split(lax.all_gather(normed_attn, "exp", axis=0, tiled=True), exp_count)
        groups = [blocks[at : at + 2] for at in range(0, exp_count, 2)]
        names = [[at, at + 1] for at in range(0, exp_count, 2)]
        out_blocks = jnp.split(lax.all_gather(w_out, "exp", axis=0, tiled=True), exp_count)
    attended, new_kv = attention(
        place,
        groups,
        names,
        (w_query, w_keyval),
        positions,
        (k_pool, v_pool),
        (pre_pos, dec_len, dec_pages, pre_pages),
        earlier,
    )
    if quick:
        attended = after(attended, pieces[1], out_blocks)
        pairs = jnp.split(attended, exp_count // 2)
        heads = [pairs[0]] + [swap(pairs[at], 2 * at) for at in range(1, exp_count // 2)]
        own, other = project(heads, out_blocks, local_rows)
        residual, normed_moe = close(hidden, moe_gain, [own, swap(other, 1)])
        mixed = plane_experts(
            normed_moe, residual, near_gates, near_places, pieces, capacity
        )
    else:
        heads = jnp.split(
            lax.all_to_all(attended, "exp", split_axis=0, concat_axis=0, tiled=True), exp_count
        )
        own, _ = project([jnp.tile(head, (2, 1)) for head in heads], out_blocks, local_rows)
        residual, normed_moe = close(hidden, moe_gain, [own])
        gates = jax.nn.softmax(router_logits, axis=-1)
        moe_out = sparse_experts(normed_moe, expert_ids, gates, w_in, w_down)
        mixed = (residual.astype(jnp.float32) + moe_out).astype(jnp.bfloat16)
    return (mixed, new_kv)


def solution(mesh):
    placed = (
        P(("req", "exp"), None),
        P(),
        P(None, "exp"),
        P(None, None, "exp"),
        P("req", None, "exp"),
        P("req", None, "exp"),
        P("req"),
        P("req", None),
        P("req"),
        P("req", None),
        P("exp", None),
        P(),
        P(("req", "exp"), None),
        P(("req", "exp"), None),
        P(("req", "exp"), None, None),
        P(("req", "exp"), None, None),
    )
    return jax.shard_map(
        body,
        mesh=mesh,
        in_specs=placed,
        out_specs=(P(("req", "exp"), None), P(None, "req", "exp")),
        check_vma=False,
    )
```

```python
import functools
import math

import jax
import jax.numpy as jnp
from jax import lax
from jax.experimental import pallas as pl
from jax.experimental.pallas import tpu as pltpu
from jax.sharding import PartitionSpec as P

HD = 128
SPLIT = 2


EPSILON = 1e-05
THETA = 10000.0


WIDE = jnp.float32


def swap(values, bits):
    count = lax.axis_size("exp")
    return lax.ppermute(values, "exp", [(d, d ^ bits) for d in range(count)])


def shift(values, steps):
    count = lax.axis_size("req")
    return lax.ppermute(values, "req", [(d, (d + steps) % count) for d in range(count)])


def after(values, *others):
    return lax.optimization_barrier((values, *others))[0]


def experts_kernel(part, wide, *refs):
    blocks, (own_in, own_down, pair_in, pair_down) = refs[:4], refs[4:8]
    outs = refs[8:12]
    rows_s, in_s, down_s, active_s, made_s, block_sem, in_sem, down_sem, out_sem = refs[12:]
    units, width = own_down.shape
    size = blocks[0].shape[0]
    parts, tiles = units // part, width // wide

    loads = [
        pltpu.make_async_copy(block, rows_s.at[pl.ds(at * size, size)], block_sem.at[at])
        for at, block in enumerate(blocks)
    ]
    arrivals = []
    for piece, weight in enumerate((own_in, pair_in)):
        for at in range(parts):
            number = piece * parts + at
            here = pl.ds(number * 2 * part, part), pl.ds((number * 2 + 1) * part, part)
            arrivals.append(
                [
                    pltpu.make_async_copy(
                        weight.at[:, pl.ds(half * units + at * part, part)],
                        in_s.at[:, here[half]],
                        in_sem.at[2 * number + half],
                    )
                    for half in range(2)
                ]
            )
    downs = [
        pltpu.make_async_copy(weight, down_s.at[pl.ds(piece * units, units)], down_sem.at[piece])
        for piece, weight in enumerate((own_down, pair_down))
    ]
    for copy in loads:
        copy.start()
    for pair in arrivals:
        for copy in pair:
            copy.start()
    for copy in downs:
        copy.start()
    for copy in loads:
        copy.wait()
    rows = rows_s[...]
    for number, pair in enumerate(arrivals):
        for copy in pair:
            copy.wait()
        both = jnp.dot(
            rows,
            in_s[:, 2 * part * number : 2 * part * (number + 1)],
            preferred_element_type=WIDE,
        )
        gate, up = both[:, :part], both[:, part:]
        active = gate / (1.0 + jnp.exp(-gate)) * up
        active_s[:, part * number : part * (number + 1)] = active.astype(jnp.bfloat16)
    for copy in downs:
        copy.wait()
    active = active_s[...]
    stores = []
    for tile in range(tiles):
        here = slice(tile * wide, (tile + 1) * wide)
        made = jnp.dot(active, down_s[:, here], preferred_element_type=WIDE)
        for at, out in enumerate(outs):
            mine = slice(at * size, (at + 1) * size)
            made_s[mine, here] = made[mine].astype(jnp.bfloat16)
            copy = pltpu.make_async_copy(
                made_s.at[pl.ds(at * size, size), pl.ds(tile * wide, wide)],
                out.at[:, pl.ds(tile * wide, wide)],
                out_sem.at[tile * len(outs) + at],
            )
            copy.start()
            stores.append(copy)
    for copy in stores:
        copy.wait()


def expert_rows(blocks, pieces):
    (own_in, own_down), (pair_in, pair_down) = pieces
    units, width = own_down.shape
    size, count = blocks[0].shape[0], len(blocks)
    rows = size * count
    part, wide = math.gcd(units, 256), math.gcd(width, 512)
    apart = pl.BlockSpec(memory_space=pl.ANY)
    return pl.pallas_call(
        functools.partial(experts_kernel, part, wide),
        out_shape=[jax.ShapeDtypeStruct((size, width), jnp.bfloat16)] * count,
        in_specs=[apart] * (count + 4),
        out_specs=[apart] * count,
        scratch_shapes=[
            pltpu.VMEM((rows, width), jnp.bfloat16),
            pltpu.VMEM((width, 4 * units), jnp.bfloat16),
            pltpu.VMEM((2 * units, width), jnp.bfloat16),
            pltpu.VMEM((rows, 2 * units), jnp.bfloat16),
            pltpu.VMEM((rows, width), jnp.bfloat16),
            pltpu.SemaphoreType.DMA((count,)),
            pltpu.SemaphoreType.DMA((4 * (units // part),)),
            pltpu.SemaphoreType.DMA((2,)),
            pltpu.SemaphoreType.DMA((count * (width // wide),)),
        ],
        compiler_params=pltpu.CompilerParams(vmem_limit_bytes=30 * MIB),
        cost_estimate=pl.CostEstimate(
            flops=12 * rows * width * units,
            bytes_accessed=16 * MIB,
            transcendentals=2 * rows * units,
        ),
        name="experts",
    )(*blocks, own_in, own_down, pair_in, pair_down)


def pick_kernel(gate_ref, place_ref, rows_ref, *refs):
    outs, (made_s, sem) = refs[:-2], refs[-2:]
    rows = rows_ref[...]
    capacity = outs[0].shape[0]
    stores = []
    for at, out in enumerate(outs):
        room = lax.broadcasted_iota(jnp.int32, (capacity, rows.shape[0]), 0)
        chosen = jnp.logical_and(gate_ref[at : at + 1, :] > 0, place_ref[at : at + 1, :] == room)
        picked = jnp.where(chosen, 1.0, 0.0).astype(jnp.bfloat16)
        made = jnp.dot(picked, rows, preferred_element_type=WIDE).astype(jnp.bfloat16)
        made_s[at * capacity : (at + 1) * capacity, :] = made
        copy = pltpu.make_async_copy(
            made_s.at[pl.ds(at * capacity, capacity)], out, sem.at[at]
        )
        copy.start()
        stores.append(copy)
    for copy in stores:
        copy.wait()


def pick(rows, gates, places, count, capacity):
    array = pl.BlockSpec(memory_space=pltpu.VMEM)
    width = rows.shape[1]
    return pl.pallas_call(
        pick_kernel,
        out_shape=[jax.ShapeDtypeStruct((capacity, width), jnp.bfloat16)] * count,
        in_specs=[array] * 3,
        out_specs=[pl.BlockSpec(memory_space=pl.ANY)] * count,
        scratch_shapes=[
            pltpu.VMEM((count * capacity, width), jnp.bfloat16),
            pltpu.SemaphoreType.DMA((count,)),
        ],
        compiler_params=pltpu.CompilerParams(vmem_limit_bytes=12 * MIB),
        cost_estimate=pl.CostEstimate(
            flops=2 * count * capacity * rows.size, bytes_accessed=MIB, transcendentals=0
        ),
        name="pick",
    )(gates, places, rows)


def merge_kernel(count, gate_ref, place_ref, *refs):
    parts, terms, (out_ref, parts_s, sem) = refs[:count], refs[count:-3], refs[-3:]
    capacity = parts[0].shape[0]
    loads = []
    for at, part in enumerate(parts):
        here = parts_s.at[pl.ds(at * capacity, capacity)]
        loads.append(pltpu.make_async_copy(part, here, sem.at[at]))
        loads[-1].start()
    gates, places = gate_ref[...].T, place_ref[...].T
    total = 0.0
    for at in range(count):
        gate, place = gates[:, at : at + 1], places[:, at : at + 1]
        room = lax.broadcasted_iota(jnp.int32, (gates.shape[0], capacity), 1)
        chosen = jnp.logical_and(gate > 0, place == room)
        spread = jnp.where(chosen, 1.0, 0.0).astype(jnp.bfloat16)
        loads[at].wait()
        part = parts_s[at * capacity : (at + 1) * capacity, :]
        total = total + gate * jnp.dot(spread, part, preferred_element_type=WIDE)
    for term in terms:
        total = total + term[...].astype(WIDE)
    out_ref[...] = total.astype(jnp.bfloat16)


def merge(parts, gates, places, terms):
    array = pl.BlockSpec(memory_space=pltpu.VMEM)
    count, (capacity, width) = len(parts), parts[0].shape
    rows = gates.shape[1]
    return pl.pallas_call(
        functools.partial(merge_kernel, count),
        out_shape=jax.ShapeDtypeStruct((rows, width), jnp.bfloat16),
        in_specs=[array] * 2
        + [pl.BlockSpec(memory_space=pl.ANY)] * count
        + [array] * len(terms),
        out_specs=array,
        scratch_shapes=[
            pltpu.VMEM((count * capacity, width), jnp.bfloat16),
            pltpu.SemaphoreType.DMA((count,)),
        ],
        compiler_params=pltpu.CompilerParams(vmem_limit_bytes=16 * MIB),
        cost_estimate=pl.CostEstimate(
            flops=2 * rows * width * count * capacity, bytes_accessed=MIB, transcendentals=0
        ),
        name="merge",
    )(gates, places, *parts, *terms)


def plane_experts(normed_moe, residual, gates, places, pieces, capacity):
    steps = lax.axis_size("req")
    count = lax.axis_size("exp") // 2
    def exchange(parts, *earlier):
        mine, *others = parts
        others = after(tuple(others), *earlier)
        return [mine, *(swap(part, 2 * at) for at, part in enumerate(others, 1))]

    def use(step):
        return pick(moved[step], gates[step], places[step], count, capacity)

    moved = [normed_moe]
    came = [exchange(use(0))]
    made, back, chain = [], [], []
    for step in range(1, steps):
        moved.append(shift(moved[-1], 1))
        if step == 1:
            moved[1] = after(moved[1], came[0])
    for step in range(1, steps):
        made.append(expert_rows(after(came[step - 1], *made[-1:]), pieces))
        if step > 2:
            back.append(exchange(made[step - 2]))
        came.append(exchange(use(step), *came[step - 2 : step - 1]))
    made.append(expert_rows(after(came[-1], made[-1]), pieces))
    for step in range(1, steps):
        if step >= len(back) + 1:
            back.append(exchange(made[step], *back[step - 2 : step - 1]))
        chain = [merge(back[step - 1], gates[step], places[step], chain)]
        chain = [shift(chain[0], 1)]
    last = exchange(made[0], *back[-2:-1])
    return merge(last, gates[0], places[0], [*chain, residual])


LOW = -1e30
MIB = 1 << 20


def rope_tables(positions):
    half = HD // 2
    steps = jnp.arange(half, dtype=WIDE)
    frequency = jnp.exp(steps * (-2.0 * math.log(THETA) / HD))
    angles = positions.astype(WIDE)[:, None] * frequency[None, :]
    cosine, sine = jnp.cos(angles), jnp.sin(angles)
    return (
        jnp.concatenate([cosine, cosine], axis=1),
        jnp.concatenate([-sine, sine], axis=1),
    )


def dot_rows(left, right):
    return lax.dot_general(left, right, (((1,), (1,)), ((), ())), preferred_element_type=WIDE)


def attention_kernel(layout, block_rows, tile, *refs):
    ref_count = sum(count for count, _ in layout)
    place_ref, length_ref, limits_ref, dec_pages_ref, pre_pages_ref = refs[:5]
    sources = refs[5 : 5 + ref_count]
    w_query, w_keyval, same_ref, other_ref, k_pool, v_pool, _, out_ref, kv_ref = refs[
        5 + ref_count : 14 + ref_count
    ]
    (rows_s, weight_s, query_s, turned_s, pre_k, pre_v, dec_k, dec_v) = refs[
        14 + ref_count : 22 + ref_count
    ]
    row_sem, weight_sem, pre_sem, dec_sem = refs[22 + ref_count :]
    page_size = k_pool.shape[1]
    dec_count, dec_pages = dec_pages_ref.shape
    pre_pages = pre_pages_ref.shape[1]
    pre_keys = pre_pages * page_size
    rows = query_s.shape[0]
    dec_keys = dec_pages * page_size
    place = place_ref[0]
    length = length_ref[0]
    rate = math.log2(math.e) / math.sqrt(HD)

    weight_copies = [
        pltpu.make_async_copy(part, weight_s.at[:, pl.ds(at * HD, HD)], weight_sem.at[at])
        for at, part in enumerate((w_query, w_keyval.at[0], w_keyval.at[1]))
    ]
    row_copies, start = [], 0
    for at, source in enumerate(sources):
        here = rows_s.at[pl.ds(start, source.shape[0])]
        row_copies.append(pltpu.make_async_copy(source, here, row_sem.at[at]))
        start += source.shape[0]
    for copy in weight_copies + row_copies:
        copy.start()

    def fetch_prefix(at, carry):
        page = pre_pages_ref[0, at]
        here = pl.ds(pl.multiple_of(at * page_size, page_size), page_size)
        pltpu.make_async_copy(k_pool.at[page], pre_k.at[here], pre_sem.at[0]).start()
        pltpu.make_async_copy(v_pool.at[page], pre_v.at[here], pre_sem.at[1]).start()
        return carry

    lax.fori_loop(0, pre_pages, fetch_prefix, 0)
    for request in range(dec_count):

        def fetch_decode(at, carry):
            page = dec_pages_ref[request, at]
            here = pl.ds(pl.multiple_of(at * page_size, page_size), page_size)
            pltpu.make_async_copy(
                k_pool.at[page], dec_k.at[request, here], dec_sem.at[0, request]
            ).start()
            pltpu.make_async_copy(
                v_pool.at[page], dec_v.at[request, here], dec_sem.at[1, request]
            ).start()
            return carry

        lax.fori_loop(0, dec_pages, fetch_decode, 0)

    for copy in weight_copies:
        copy.wait()
    start = 0
    for count, names in layout:
        for _ in range(count):
            row_copies.pop(0).wait()
        size = block_rows * len(names)
        made = jnp.dot(rows_s[start : start + size], weight_s[...], preferred_element_type=WIDE)
        start += size
        for at, name in enumerate(names):
            mine = made[at * block_rows : (at + 1) * block_rows]
            first = pl.multiple_of((place ^ name) * block_rows, block_rows)
            here = pl.ds(first, block_rows)
            same, other = same_ref[here, :], other_ref[here, :]
            query, key = mine[:, :HD], mine[:, HD : 2 * HD]
            query_s[here, :] = (query * same + pltpu.roll(query, HD // 2, 1) * other).astype(
                jnp.bfloat16
            )
            kv_ref[0, here, :] = (key * same + pltpu.roll(key, HD // 2, 1) * other).astype(
                jnp.bfloat16
            )
            kv_ref[1, here, :] = mine[:, 2 * HD :].astype(jnp.bfloat16)

    pltpu.make_async_copy(pre_k, pre_k, pre_sem.at[0]).wait()
    pltpu.make_async_copy(pre_v, pre_v, pre_sem.at[1]).wait()

    turned_s[:HD, :pre_keys] = pre_v[...].T
    turned_s[:HD, pre_keys:] = kv_ref[1].T
    turned_s[HD:, :] = jnp.ones((turned_s.shape[0] - HD, turned_s.shape[1]), jnp.bfloat16)
    slots = lax.broadcasted_iota(jnp.int32, (pre_keys, 1), 0)
    bias = jnp.where(slots < length, 0.0, LOW)
    for at in range(rows // tile):
        start = at * tile
        held = start + tile
        query = query_s[start:held, :]
        scores = dot_rows(pre_k[...], query) * rate + bias
        own = dot_rows(kv_ref[0, :held, :], query) * rate
        seen = lax.broadcasted_iota(jnp.int32, own.shape, 0)
        asked = start + lax.broadcasted_iota(jnp.int32, own.shape, 1)
        own = jnp.where(jnp.logical_and(seen >= dec_count, seen <= asked), own, LOW)
        highest = jnp.maximum(
            jnp.max(scores, axis=0, keepdims=True), jnp.max(own, axis=0, keepdims=True)
        )
        weights = jnp.exp2(scores - highest).astype(jnp.bfloat16)
        own_weights = jnp.exp2(own - highest).astype(jnp.bfloat16)
        total = jnp.dot(
            turned_s[:, :pre_keys], weights, preferred_element_type=WIDE
        ) + jnp.dot(
            turned_s[:, pre_keys : pre_keys + held], own_weights, preferred_element_type=WIDE
        )
        done = (total[:HD] / total[HD : HD + 1]).T.astype(jnp.bfloat16)
        for part in range(tile // block_rows):
            target = (at * (tile // block_rows) + part) ^ place
            target = pl.multiple_of(target * block_rows, block_rows)
            out_ref[pl.ds(target, block_rows), :] = done[
                part * block_rows : (part + 1) * block_rows
            ]

    few = 16
    query = query_s[:few, :]
    row = lax.broadcasted_iota(jnp.int32, (few, HD), 0)
    own_scores = dot_rows(query, kv_ref[0, :few, :]) * rate
    first_rows = pl.ds(pl.multiple_of(place * block_rows, block_rows), few)
    result = out_ref[first_rows, :].astype(WIDE)
    for request in range(dec_count):
        pltpu.make_async_copy(dec_k.at[request], dec_k.at[request], dec_sem.at[0, request]).wait()
        pltpu.make_async_copy(dec_v.at[request], dec_v.at[request], dec_sem.at[1, request]).wait()
        scores = dot_rows(query, dec_k[request]) * rate
        slots = lax.broadcasted_iota(jnp.int32, (few, dec_keys), 1)
        scores = jnp.where(slots < limits_ref[request], scores, LOW)
        itself = lax.broadcasted_iota(jnp.int32, (few, few), 1) == request
        own = jnp.where(itself, own_scores, LOW)
        highest = jnp.maximum(
            jnp.max(scores, axis=1, keepdims=True), jnp.max(own, axis=1, keepdims=True)
        )
        weights = jnp.exp2(scores - highest)
        own_weights = jnp.exp2(own - highest)
        total = jnp.sum(weights, axis=1, keepdims=True) + jnp.sum(
            own_weights, axis=1, keepdims=True
        )
        summed = jnp.dot(
            weights.astype(jnp.bfloat16), dec_v[request], preferred_element_type=WIDE
        ) + jnp.dot(
            own_weights.astype(jnp.bfloat16), kv_ref[1, :few, :], preferred_element_type=WIDE
        )
        result = jnp.where(row == request, summed / total, result)
    out_ref[first_rows, :] = result.astype(jnp.bfloat16)


def attention(place, groups, names, weights, positions, pools, tables, earlier):
    pre_pos, dec_len, dec_pages, pre_pages = tables
    k_pool, v_pool = pools
    w_query, w_keyval = weights
    blocks = [block for group in groups for block in group]
    rows = sum(block.shape[0] for block in blocks)
    block_rows = rows // sum(len(group) for group in names)
    layout = [(len(group), name) for group, name in zip(groups, names, strict=True)]
    page_size = k_pool.shape[1]
    pre_keys = pre_pages.shape[1] * page_size
    dec_keys = dec_pages.shape[1] * page_size
    dec_count = dec_pages.shape[0]
    tile = 4 * block_rows
    width = w_query.shape[0]
    same, other = rope_tables(positions)
    number = pl.BlockSpec(memory_space=pltpu.SMEM)
    array = pl.BlockSpec(memory_space=pltpu.VMEM)
    apart = pl.BlockSpec(memory_space=pl.ANY)
    flops = 2 * rows * (3 * HD * width + 2 * HD * (pre_keys + rows))
    return pl.pallas_call(
        functools.partial(attention_kernel, layout, block_rows, tile),
        out_shape=(
            jax.ShapeDtypeStruct((rows, HD), jnp.bfloat16),
            jax.ShapeDtypeStruct((2, rows, HD), jnp.bfloat16),
        ),
        in_specs=[number] * 5 + [apart] * (len(blocks) + 2) + [array] * 2 + [apart] * 3,
        out_specs=(array, array),
        scratch_shapes=[
            pltpu.VMEM((rows, width), jnp.bfloat16),
            pltpu.VMEM((width, 3 * HD), jnp.bfloat16),
            pltpu.VMEM((rows, HD), jnp.bfloat16),
            pltpu.VMEM((HD + 16, pre_keys + rows), jnp.bfloat16),
            pltpu.VMEM((pre_keys, HD), jnp.bfloat16),
            pltpu.VMEM((pre_keys, HD), jnp.bfloat16),
            pltpu.VMEM((dec_count, dec_keys, HD), jnp.bfloat16),
            pltpu.VMEM((dec_count, dec_keys, HD), jnp.bfloat16),
            pltpu.SemaphoreType.DMA((len(blocks),)),
            pltpu.SemaphoreType.DMA((3,)),
            pltpu.SemaphoreType.DMA((2,)),
            pltpu.SemaphoreType.DMA((2, dec_count)),
        ],
        compiler_params=pltpu.CompilerParams(vmem_limit_bytes=48 * MIB),
        cost_estimate=pl.CostEstimate(
            flops=flops, bytes_accessed=20 * MIB, transcendentals=rows * (pre_keys + rows)
        ),
        name="attention",
    )(
        place,
        pre_pos,
        dec_len,
        dec_pages,
        pre_pages,
        *blocks,
        w_query,
        w_keyval,
        same,
        other,
        k_pool,
        v_pool,
        earlier,
    )


def project_kernel(count, *refs):
    heads, weights = refs[:count], refs[count : 2 * count]
    own_ref, other_ref = refs[2 * count :]
    width = weights[0].shape[1]
    rows = own_ref.shape[0]
    step = math.gcd(width, 512)
    for start in range(0, width, step):
        here = slice(start, start + step)
        total = 0.0
        for first in range(0, count, 2):
            left = jnp.concatenate([heads[first][...], heads[first + 1][...]], axis=1)
            right = jnp.concatenate(
                [weights[first][:, here], weights[first + 1][:, here]], axis=0
            )
            total = total + jnp.dot(left, right, preferred_element_type=WIDE)
        own_ref[:, here] = total[:rows]
        other_ref[:, here] = total[rows:].astype(jnp.bfloat16)


def project(heads, weights, rows):
    array = pl.BlockSpec(memory_space=pltpu.VMEM)
    count, all_rows, width = len(heads), heads[0].shape[0], weights[0].shape[1]
    return pl.pallas_call(
        functools.partial(project_kernel, count),
        out_shape=(
            jax.ShapeDtypeStruct((rows, width), WIDE),
            jax.ShapeDtypeStruct((all_rows - rows, width), jnp.bfloat16),
        ),
        in_specs=[array] * (2 * count),
        out_specs=(array, array),
        compiler_params=pltpu.CompilerParams(vmem_limit_bytes=32 * MIB),
        cost_estimate=pl.CostEstimate(
            flops=2 * all_rows * width * count * HD, bytes_accessed=4 * MIB, transcendentals=0
        ),
        name="project",
    )(*heads, *weights)


def close_kernel(hidden_ref, gain_ref, *refs):
    *terms, residual_ref, normed_ref = refs
    total = hidden_ref[...].astype(WIDE)
    for term in terms:
        total = total + term[...].astype(WIDE)
    rounded = total.astype(jnp.bfloat16)
    residual_ref[...] = rounded
    total = rounded.astype(WIDE)
    factor = lax.rsqrt(jnp.mean(total * total, axis=1, keepdims=True) + EPSILON)
    normed_ref[...] = (total * factor * gain_ref[...]).astype(jnp.bfloat16)


def close(hidden, gain, terms):
    array = pl.BlockSpec(memory_space=pltpu.VMEM)
    return pl.pallas_call(
        close_kernel,
        out_shape=(jax.ShapeDtypeStruct(hidden.shape, jnp.bfloat16),) * 2,
        in_specs=[array] * (2 + len(terms)),
        out_specs=(array, array),
        compiler_params=pltpu.CompilerParams(vmem_limit_bytes=16 * MIB),
        name="close",
    )(hidden, gain[None, :], *terms)


def norm_kernel(hidden_ref, gain_ref, out_ref):
    values = hidden_ref[...].astype(WIDE)
    factor = lax.rsqrt(jnp.mean(values * values, axis=1, keepdims=True) + EPSILON)
    out_ref[...] = (values * factor * gain_ref[...]).astype(jnp.bfloat16)


def norm(hidden, gain):
    array = pl.BlockSpec(memory_space=pltpu.VMEM)
    return pl.pallas_call(
        norm_kernel,
        out_shape=jax.ShapeDtypeStruct(hidden.shape, jnp.bfloat16),
        in_specs=[array, array],
        out_specs=array,
        compiler_params=pltpu.CompilerParams(vmem_limit_bytes=16 * MIB),
        name="norm",
    )(hidden, gain[None, :])


def gather_blocks(rows, first):
    half = rows.shape[0] // 2
    from_x, from_y = swap(rows, 2), swap(rows, 4)
    beside = swap(after(rows, from_x), 1)
    x_1, y_2 = after((from_x[:half], from_y[half:]), *first)
    far = jnp.concatenate([swap(x_1, 4), swap(y_2, 2)], axis=0)
    near = jnp.concatenate([from_x, from_y], axis=0)
    near_beside = swap(near, 1)
    return (
        [[rows, beside], [near], [near_beside], [far, swap(far, 1)]],
        [[0, 1], [2, 4], [3, 5], [6, 7]],
    )


def gate_table(expert_ids, gates):
    req_count = lax.axis_size("req")
    exp_count = lax.axis_size("exp")
    experts = req_count * exp_count // SPLIT
    named = expert_ids.T[None] == jnp.arange(experts, dtype=jnp.int32)[:, None, None]
    table = jnp.sum(jnp.where(named, gates.T[None], 0.0), axis=1)
    near = jnp.stack([table, shift(table, 1)])
    near = jnp.concatenate([near, shift(near, 2)])
    bits = jnp.arange(0, exp_count, 2, dtype=jnp.int32)
    owner = lax.axis_index("req") * exp_count + (lax.axis_index("exp") ^ bits)
    chosen = (owner // SPLIT)[:, None] == jnp.arange(experts, dtype=jnp.int32)
    mine = jnp.sum(jnp.where(chosen[None, :, :, None], near[:, None], 0.0), axis=2)
    mine = jnp.pad(mine, ((0, 0), (0, -mine.shape[1] % 8), (0, 0)))
    marks = (mine > 0).astype(jnp.int32)
    return mine, jnp.cumsum(marks, axis=2) - marks


def deliver(buffer):
    result = lax.all_to_all(buffer, ("req", "exp"), split_axis=0, concat_axis=0, tiled=True)
    return result


def bring_back(buffer):
    result = lax.all_to_all(buffer, ("req", "exp"), split_axis=0, concat_axis=0, tiled=True)
    return result


def slots_of(choices, experts):
    return 2 * ((choices * 5 + 8 * experts - 1) // (8 * experts))


def sparse_experts(normed_moe, expert_ids, gates, w_in, w_down):
    local_rows, width = normed_moe.shape
    devices = lax.axis_size("req") * lax.axis_size("exp")
    experts = devices // SPLIT
    top = expert_ids.shape[1]
    capacity = slots_of(local_rows * top, experts)
    assigned = expert_ids.reshape(-1)
    count_all = assigned.shape[0]
    marks = (assigned[:, None] == jnp.arange(experts, dtype=jnp.int32)[None, :]).astype(jnp.int32)
    earlier = jnp.cumsum(marks, axis=0) - marks
    place = jnp.sum(earlier * marks, axis=1)
    target = assigned * capacity + place
    owner_rows = jnp.arange(count_all, dtype=jnp.int32) // top
    outgoing = (
        jnp.zeros((experts * capacity, width), jnp.bfloat16).at[target].set(normed_moe[owner_rows])
    )
    doubled = jnp.broadcast_to(
        outgoing.reshape(experts, 1, capacity, width), (experts, SPLIT, capacity, width)
    ).reshape(devices, capacity, width)
    arrived = deliver(doubled)
    piece_units = w_down.shape[1]
    inner = jnp.dot(
        arrived.reshape(devices * capacity, width), w_in[0], preferred_element_type=jnp.float32
    )
    activated = (jax.nn.silu(inner[:, :piece_units]) * inner[:, piece_units:]).astype(jnp.bfloat16)
    partial_value = (
        jnp.dot(activated, w_down[0], preferred_element_type=jnp.float32)
        .astype(jnp.bfloat16)
        .reshape(devices, capacity, width)
    )
    returned = bring_back(partial_value).reshape(devices * capacity, width)
    base_index = assigned * (SPLIT * capacity) + place
    lower_half = returned[base_index].astype(jnp.float32)
    upper_half = returned[base_index + capacity].astype(jnp.float32)
    weighted = (lower_half + upper_half) * gates.reshape(-1)[:, None]
    moe_out = jnp.sum(weighted.reshape(local_rows, top, width), axis=1)
    return moe_out


def body(
    hidden,
    attn_gain,
    w_query,
    w_keyval,
    k_pool,
    v_pool,
    dec_len,
    dec_pages,
    pre_pos,
    pre_pages,
    w_out,
    moe_gain,
    expert_ids,
    router_logits,
    w_in,
    w_down,
):
    local_rows, width = hidden.shape
    exp_count = lax.axis_size("exp")
    group_rows = local_rows * exp_count
    dec_count = dec_len.shape[0]
    quick = exp_count == 8
    experts = lax.axis_size("req") * exp_count // SPLIT
    capacity = slots_of(local_rows * expert_ids.shape[1], experts)
    normed_attn = norm(hidden, attn_gain)
    row_index = jnp.arange(group_rows, dtype=jnp.int32)
    own_positions = jnp.sum(
        jnp.where(row_index[:, None] == jnp.arange(dec_count), dec_len[None, :], 0), axis=1
    )
    positions = jnp.where(row_index < dec_count, own_positions, pre_pos[0] + row_index - dec_count)
    if quick:
        place = lax.axis_index("exp").reshape(1)
        gates = jax.nn.softmax(router_logits, axis=-1)
        near_gates, near_places = gate_table(expert_ids, gates)
        own_in, own_down = w_in[0], w_down[0]
        pair_in = swap(own_in, 1)
        groups, names = gather_blocks(normed_attn, (near_places, pair_in))
        far, late = groups[-1]
        own_out, late_down = after(w_out, far), after(own_down, late)
        out_blocks = [w_out] + [swap(own_out, bits) for bits in (2, 4, 6)]
        pieces = [(own_in, own_down), (pair_in, swap(late_down, 1))]
        earlier = near_places
    else:
        place = jnp.zeros((1,), jnp.int32)
        earlier = place
        blocks = jnp.split(lax.all_gather(normed_attn, "exp", axis=0, tiled=True), exp_count)
        groups = [blocks[at : at + 2] for at in range(0, exp_count, 2)]
        names = [[at, at + 1] for at in range(0, exp_count, 2)]
        out_blocks = jnp.split(lax.all_gather(w_out, "exp", axis=0, tiled=True), exp_count)
    attended, new_kv = attention(
        place,
        groups,
        names,
        (w_query, w_keyval),
        positions,
        (k_pool, v_pool),
        (pre_pos, dec_len, dec_pages, pre_pages),
        earlier,
    )
    if quick:
        attended = after(attended, pieces[1], out_blocks)
        pairs = jnp.split(attended, exp_count // 2)
        heads = [pairs[0]] + [swap(pairs[at], 2 * at) for at in range(1, exp_count // 2)]
        own, other = project(heads, out_blocks, local_rows)
        residual, normed_moe = close(hidden, moe_gain, [own, swap(other, 1)])
        mixed = plane_experts(
            normed_moe, residual, near_gates, near_places, pieces, capacity
        )
    else:
        heads = jnp.split(
            lax.all_to_all(attended, "exp", split_axis=0, concat_axis=0, tiled=True), exp_count
        )
        own, _ = project([jnp.tile(head, (2, 1)) for head in heads], out_blocks, local_rows)
        residual, normed_moe = close(hidden, moe_gain, [own])
        gates = jax.nn.softmax(router_logits, axis=-1)
        moe_out = sparse_experts(normed_moe, expert_ids, gates, w_in, w_down)
        mixed = (residual.astype(jnp.float32) + moe_out).astype(jnp.bfloat16)
    return (mixed, new_kv)


def solution(mesh):
    placed = (
        P(("req", "exp"), None),
        P(),
        P(None, "exp"),
        P(None, None, "exp"),
        P("req", None, "exp"),
        P("req", None, "exp"),
        P("req"),
        P("req", None),
        P("req"),
        P("req", None),
        P("exp", None),
        P(),
        P(("req", "exp"), None),
        P(("req", "exp"), None),
        P(("req", "exp"), None, None),
        P(("req", "exp"), None, None),
    )
    return jax.shard_map(
        body,
        mesh=mesh,
        in_specs=placed,
        out_specs=(P(("req", "exp"), None), P(None, "req", "exp")),
        check_vma=False,
    )
```

```python
import functools
import math

import jax
import jax.numpy as jnp
from jax import lax
from jax.experimental import pallas as pl
from jax.experimental.pallas import tpu as pltpu
from jax.sharding import PartitionSpec as P

HD = 128
SPLIT = 2


EPSILON = 1e-05
THETA = 10000.0


WIDE = jnp.float32


def swap(values, bits):
    count = lax.axis_size("exp")
    return lax.ppermute(values, "exp", [(d, d ^ bits) for d in range(count)])


def shift(values, steps):
    count = lax.axis_size("req")
    return lax.ppermute(values, "req", [(d, (d + steps) % count) for d in range(count)])


def after(values, *others):
    return lax.optimization_barrier((values, *others))[0]


def experts_kernel(part, wide, *refs):
    blocks, (own_in, own_down, pair_in, pair_down) = refs[:4], refs[4:8]
    outs = refs[8:12]
    rows_s, in_s, down_s, active_s, made_s, block_sem, in_sem, down_sem, out_sem = refs[12:]
    units, width = own_down.shape
    size = blocks[0].shape[0]
    parts, tiles = units // part, width // wide

    loads = [
        pltpu.make_async_copy(block, rows_s.at[pl.ds(at * size, size)], block_sem.at[at])
        for at, block in enumerate(blocks)
    ]
    arrivals = []
    for piece, weight in enumerate((own_in, pair_in)):
        for at in range(parts):
            number = piece * parts + at
            here = pl.ds(number * 2 * part, part), pl.ds((number * 2 + 1) * part, part)
            arrivals.append(
                [
                    pltpu.make_async_copy(
                        weight.at[:, pl.ds(half * units + at * part, part)],
                        in_s.at[:, here[half]],
                        in_sem.at[2 * number + half],
                    )
                    for half in range(2)
                ]
            )
    downs = [
        pltpu.make_async_copy(weight, down_s.at[pl.ds(piece * units, units)], down_sem.at[piece])
        for piece, weight in enumerate((own_down, pair_down))
    ]
    for copy in loads:
        copy.start()
    for pair in arrivals:
        for copy in pair:
            copy.start()
    for copy in downs:
        copy.start()
    for copy in loads:
        copy.wait()
    rows = rows_s[...]
    for number, pair in enumerate(arrivals):
        for copy in pair:
            copy.wait()
        both = jnp.dot(
            rows,
            in_s[:, 2 * part * number : 2 * part * (number + 1)],
            preferred_element_type=WIDE,
        )
        gate, up = both[:, :part], both[:, part:]
        active = gate / (1.0 + jnp.exp(-gate)) * up
        active_s[:, part * number : part * (number + 1)] = active.astype(jnp.bfloat16)
    for copy in downs:
        copy.wait()
    active = active_s[...]
    stores = []
    for tile in range(tiles):
        here = slice(tile * wide, (tile + 1) * wide)
        made = jnp.dot(active, down_s[:, here], preferred_element_type=WIDE)
        for at, out in enumerate(outs):
            mine = slice(at * size, (at + 1) * size)
            made_s[mine, here] = made[mine].astype(jnp.bfloat16)
            copy = pltpu.make_async_copy(
                made_s.at[pl.ds(at * size, size), pl.ds(tile * wide, wide)],
                out.at[:, pl.ds(tile * wide, wide)],
                out_sem.at[tile * len(outs) + at],
            )
            copy.start()
            stores.append(copy)
    for copy in stores:
        copy.wait()


def expert_rows(blocks, pieces):
    (own_in, own_down), (pair_in, pair_down) = pieces
    units, width = own_down.shape
    size, count = blocks[0].shape[0], len(blocks)
    rows = size * count
    part, wide = math.gcd(units, 256), math.gcd(width, 512)
    apart = pl.BlockSpec(memory_space=pl.ANY)
    return pl.pallas_call(
        functools.partial(experts_kernel, part, wide),
        out_shape=[jax.ShapeDtypeStruct((size, width), jnp.bfloat16)] * count,
        in_specs=[apart] * (count + 4),
        out_specs=[apart] * count,
        scratch_shapes=[
            pltpu.VMEM((rows, width), jnp.bfloat16),
            pltpu.VMEM((width, 4 * units), jnp.bfloat16),
            pltpu.VMEM((2 * units, width), jnp.bfloat16),
            pltpu.VMEM((rows, 2 * units), jnp.bfloat16),
            pltpu.VMEM((rows, width), jnp.bfloat16),
            pltpu.SemaphoreType.DMA((count,)),
            pltpu.SemaphoreType.DMA((4 * (units // part),)),
            pltpu.SemaphoreType.DMA((2,)),
            pltpu.SemaphoreType.DMA((count * (width // wide),)),
        ],
        compiler_params=pltpu.CompilerParams(vmem_limit_bytes=30 * MIB),
        cost_estimate=pl.CostEstimate(
            flops=12 * rows * width * units,
            bytes_accessed=16 * MIB,
            transcendentals=2 * rows * units,
        ),
        name="experts",
    )(*blocks, own_in, own_down, pair_in, pair_down)


def pick_kernel(gate_ref, place_ref, rows_ref, *refs):
    outs, (made_s, sem) = refs[:-2], refs[-2:]
    rows = rows_ref[...]
    capacity = outs[0].shape[0]
    stores = []
    for at, out in enumerate(outs):
        room = lax.broadcasted_iota(jnp.int32, (capacity, rows.shape[0]), 0)
        chosen = jnp.logical_and(gate_ref[at : at + 1, :] > 0, place_ref[at : at + 1, :] == room)
        picked = jnp.where(chosen, 1.0, 0.0).astype(jnp.bfloat16)
        made = jnp.dot(picked, rows, preferred_element_type=WIDE).astype(jnp.bfloat16)
        made_s[at * capacity : (at + 1) * capacity, :] = made
        copy = pltpu.make_async_copy(
            made_s.at[pl.ds(at * capacity, capacity)], out, sem.at[at]
        )
        copy.start()
        stores.append(copy)
    for copy in stores:
        copy.wait()


def pick(rows, gates, places, count, capacity):
    array = pl.BlockSpec(memory_space=pltpu.VMEM)
    width = rows.shape[1]
    return pl.pallas_call(
        pick_kernel,
        out_shape=[jax.ShapeDtypeStruct((capacity, width), jnp.bfloat16)] * count,
        in_specs=[array] * 3,
        out_specs=[pl.BlockSpec(memory_space=pl.ANY)] * count,
        scratch_shapes=[
            pltpu.VMEM((count * capacity, width), jnp.bfloat16),
            pltpu.SemaphoreType.DMA((count,)),
        ],
        compiler_params=pltpu.CompilerParams(vmem_limit_bytes=12 * MIB),
        cost_estimate=pl.CostEstimate(
            flops=2 * count * capacity * rows.size, bytes_accessed=MIB, transcendentals=0
        ),
        name="pick",
    )(gates, places, rows)


def merge_kernel(count, gate_ref, place_ref, *refs):
    parts, terms, (out_ref, parts_s, sem) = refs[:count], refs[count:-3], refs[-3:]
    capacity = parts[0].shape[0]
    loads = []
    for at, part in enumerate(parts):
        here = parts_s.at[pl.ds(at * capacity, capacity)]
        loads.append(pltpu.make_async_copy(part, here, sem.at[at]))
        loads[-1].start()
    gates, places = gate_ref[...].T, place_ref[...].T
    total = 0.0
    for at in range(count):
        gate, place = gates[:, at : at + 1], places[:, at : at + 1]
        room = lax.broadcasted_iota(jnp.int32, (gates.shape[0], capacity), 1)
        chosen = jnp.logical_and(gate > 0, place == room)
        spread = jnp.where(chosen, 1.0, 0.0).astype(jnp.bfloat16)
        loads[at].wait()
        part = parts_s[at * capacity : (at + 1) * capacity, :]
        total = total + gate * jnp.dot(spread, part, preferred_element_type=WIDE)
    for term in terms:
        total = total + term[...].astype(WIDE)
    out_ref[...] = total.astype(jnp.bfloat16)


def merge(parts, gates, places, terms):
    array = pl.BlockSpec(memory_space=pltpu.VMEM)
    count, (capacity, width) = len(parts), parts[0].shape
    rows = gates.shape[1]
    return pl.pallas_call(
        functools.partial(merge_kernel, count),
        out_shape=jax.ShapeDtypeStruct((rows, width), jnp.bfloat16),
        in_specs=[array] * 2
        + [pl.BlockSpec(memory_space=pl.ANY)] * count
        + [array] * len(terms),
        out_specs=array,
        scratch_shapes=[
            pltpu.VMEM((count * capacity, width), jnp.bfloat16),
            pltpu.SemaphoreType.DMA((count,)),
        ],
        compiler_params=pltpu.CompilerParams(vmem_limit_bytes=16 * MIB),
        cost_estimate=pl.CostEstimate(
            flops=2 * rows * width * count * capacity, bytes_accessed=MIB, transcendentals=0
        ),
        name="merge",
    )(gates, places, *parts, *terms)


def plane_experts(normed_moe, residual, gates, places, pieces, capacity):
    steps = lax.axis_size("req")
    count = lax.axis_size("exp") // 2
    def exchange(parts, *earlier):
        mine, *others = parts
        others = after(tuple(others), *earlier)
        return [mine, *(swap(part, 2 * at) for at, part in enumerate(others, 1))]

    def use(step):
        return pick(moved[step], gates[step], places[step], count, capacity)

    moved = [normed_moe]
    came = [exchange(use(0))]
    made, back, chain = [], [], []
    for step in range(1, steps):
        moved.append(shift(moved[-1], 1))
        if step == 1:
            moved[1] = after(moved[1], came[0])
    for step in range(1, steps):
        made.append(expert_rows(after(came[step - 1], *made[-1:]), pieces))
        if step > 2:
            back.append(exchange(made[step - 2]))
        came.append(exchange(use(step), *came[step - 2 : step - 1]))
    made.append(expert_rows(after(came[-1], made[-1]), pieces))
    for step in range(1, steps):
        if step >= len(back) + 1:
            back.append(exchange(made[step], *back[step - 2 : step - 1]))
        chain = [merge(back[step - 1], gates[step], places[step], chain)]
        chain = [shift(chain[0], 1)]
    last = exchange(made[0], *back[-2:-1])
    return merge(last, gates[0], places[0], [*chain, residual])


LOW = -1e30
MIB = 1 << 20


def rope_tables(positions):
    half = HD // 2
    steps = jnp.arange(half, dtype=WIDE)
    frequency = jnp.exp(steps * (-2.0 * math.log(THETA) / HD))
    angles = positions.astype(WIDE)[:, None] * frequency[None, :]
    cosine, sine = jnp.cos(angles), jnp.sin(angles)
    return (
        jnp.concatenate([cosine, cosine], axis=1),
        jnp.concatenate([-sine, sine], axis=1),
    )


def dot_rows(left, right):
    return lax.dot_general(left, right, (((1,), (1,)), ((), ())), preferred_element_type=WIDE)


def attention_kernel(layout, block_rows, tile, *refs):
    ref_count = sum(count for count, _ in layout)
    place_ref, length_ref, limits_ref, dec_pages_ref, pre_pages_ref = refs[:5]
    sources = refs[5 : 5 + ref_count]
    w_query, w_keyval, same_ref, other_ref, k_pool, v_pool, _, out_ref, kv_ref = refs[
        5 + ref_count : 14 + ref_count
    ]
    (rows_s, weight_s, query_s, turned_s, pre_k, pre_v, dec_k, dec_v) = refs[
        14 + ref_count : 22 + ref_count
    ]
    row_sem, weight_sem, pre_sem, dec_sem = refs[22 + ref_count :]
    page_size = k_pool.shape[1]
    dec_count, dec_pages = dec_pages_ref.shape
    pre_pages = pre_pages_ref.shape[1]
    pre_keys = pre_pages * page_size
    rows = query_s.shape[0]
    dec_keys = dec_pages * page_size
    place = place_ref[0]
    length = length_ref[0]
    rate = math.log2(math.e) / math.sqrt(HD)

    weight_copies = [
        pltpu.make_async_copy(part, weight_s.at[:, pl.ds(at * HD, HD)], weight_sem.at[at])
        for at, part in enumerate((w_query, w_keyval.at[0], w_keyval.at[1]))
    ]
    row_copies, start = [], 0
    for at, source in enumerate(sources):
        here = rows_s.at[pl.ds(start, source.shape[0])]
        row_copies.append(pltpu.make_async_copy(source, here, row_sem.at[at]))
        start += source.shape[0]
    for copy in weight_copies + row_copies:
        copy.start()

    def fetch_prefix(at, carry):
        page = pre_pages_ref[0, at]
        here = pl.ds(pl.multiple_of(at * page_size, page_size), page_size)
        pltpu.make_async_copy(k_pool.at[page], pre_k.at[here], pre_sem.at[0]).start()
        pltpu.make_async_copy(v_pool.at[page], pre_v.at[here], pre_sem.at[1]).start()
        return carry

    lax.fori_loop(0, pre_pages, fetch_prefix, 0)
    for request in range(dec_count):

        def fetch_decode(at, carry):
            page = dec_pages_ref[request, at]
            here = pl.ds(pl.multiple_of(at * page_size, page_size), page_size)
            pltpu.make_async_copy(
                k_pool.at[page], dec_k.at[request, here], dec_sem.at[0, request]
            ).start()
            pltpu.make_async_copy(
                v_pool.at[page], dec_v.at[request, here], dec_sem.at[1, request]
            ).start()
            return carry

        lax.fori_loop(0, dec_pages, fetch_decode, 0)

    for copy in weight_copies:
        copy.wait()
    start = 0
    for count, names in layout:
        for _ in range(count):
            row_copies.pop(0).wait()
        size = block_rows * len(names)
        made = jnp.dot(rows_s[start : start + size], weight_s[...], preferred_element_type=WIDE)
        start += size
        for at, name in enumerate(names):
            mine = made[at * block_rows : (at + 1) * block_rows]
            first = pl.multiple_of((place ^ name) * block_rows, block_rows)
            here = pl.ds(first, block_rows)
            same, other = same_ref[here, :], other_ref[here, :]
            query, key = mine[:, :HD], mine[:, HD : 2 * HD]
            query_s[here, :] = (query * same + pltpu.roll(query, HD // 2, 1) * other).astype(
                jnp.bfloat16
            )
            kv_ref[0, here, :] = (key * same + pltpu.roll(key, HD // 2, 1) * other).astype(
                jnp.bfloat16
            )
            kv_ref[1, here, :] = mine[:, 2 * HD :].astype(jnp.bfloat16)

    pltpu.make_async_copy(pre_k, pre_k, pre_sem.at[0]).wait()
    pltpu.make_async_copy(pre_v, pre_v, pre_sem.at[1]).wait()

    turned_s[:HD, :pre_keys] = pre_v[...].T
    turned_s[:HD, pre_keys:] = kv_ref[1].T
    turned_s[HD:, :] = jnp.ones((turned_s.shape[0] - HD, turned_s.shape[1]), jnp.bfloat16)
    slots = lax.broadcasted_iota(jnp.int32, (pre_keys, 1), 0)
    bias = jnp.where(slots < length, 0.0, LOW)
    for at in range(rows // tile):
        start = at * tile
        held = start + tile
        query = query_s[start:held, :]
        scores = dot_rows(pre_k[...], query) * rate + bias
        own = dot_rows(kv_ref[0, :held, :], query) * rate
        seen = lax.broadcasted_iota(jnp.int32, own.shape, 0)
        asked = start + lax.broadcasted_iota(jnp.int32, own.shape, 1)
        own = jnp.where(jnp.logical_and(seen >= dec_count, seen <= asked), own, LOW)
        highest = jnp.maximum(
            jnp.max(scores, axis=0, keepdims=True), jnp.max(own, axis=0, keepdims=True)
        )
        weights = jnp.exp2(scores - highest).astype(jnp.bfloat16)
        own_weights = jnp.exp2(own - highest).astype(jnp.bfloat16)
        total = jnp.dot(
            turned_s[:, :pre_keys], weights, preferred_element_type=WIDE
        ) + jnp.dot(
            turned_s[:, pre_keys : pre_keys + held], own_weights, preferred_element_type=WIDE
        )
        done = (total[:HD] / total[HD : HD + 1]).T.astype(jnp.bfloat16)
        for part in range(tile // block_rows):
            target = (at * (tile // block_rows) + part) ^ place
            target = pl.multiple_of(target * block_rows, block_rows)
            out_ref[pl.ds(target, block_rows), :] = done[
                part * block_rows : (part + 1) * block_rows
            ]

    few = 16
    query = query_s[:few, :]
    row = lax.broadcasted_iota(jnp.int32, (few, HD), 0)
    own_scores = dot_rows(query, kv_ref[0, :few, :]) * rate
    first_rows = pl.ds(pl.multiple_of(place * block_rows, block_rows), few)
    result = out_ref[first_rows, :].astype(WIDE)
    for request in range(dec_count):
        pltpu.make_async_copy(dec_k.at[request], dec_k.at[request], dec_sem.at[0, request]).wait()
        pltpu.make_async_copy(dec_v.at[request], dec_v.at[request], dec_sem.at[1, request]).wait()
        scores = dot_rows(query, dec_k[request]) * rate
        slots = lax.broadcasted_iota(jnp.int32, (few, dec_keys), 1)
        scores = jnp.where(slots < limits_ref[request], scores, LOW)
        itself = lax.broadcasted_iota(jnp.int32, (few, few), 1) == request
        own = jnp.where(itself, own_scores, LOW)
        highest = jnp.maximum(
            jnp.max(scores, axis=1, keepdims=True), jnp.max(own, axis=1, keepdims=True)
        )
        weights = jnp.exp2(scores - highest)
        own_weights = jnp.exp2(own - highest)
        total = jnp.sum(weights, axis=1, keepdims=True) + jnp.sum(
            own_weights, axis=1, keepdims=True
        )
        summed = jnp.dot(
            weights.astype(jnp.bfloat16), dec_v[request], preferred_element_type=WIDE
        ) + jnp.dot(
            own_weights.astype(jnp.bfloat16), kv_ref[1, :few, :], preferred_element_type=WIDE
        )
        result = jnp.where(row == request, summed / total, result)
    out_ref[first_rows, :] = result.astype(jnp.bfloat16)


def attention(place, groups, names, weights, positions, pools, tables, earlier):
    pre_pos, dec_len, dec_pages, pre_pages = tables
    k_pool, v_pool = pools
    w_query, w_keyval = weights
    blocks = [block for group in groups for block in group]
    rows = sum(block.shape[0] for block in blocks)
    block_rows = rows // sum(len(group) for group in names)
    layout = [(len(group), name) for group, name in zip(groups, names, strict=True)]
    page_size = k_pool.shape[1]
    pre_keys = pre_pages.shape[1] * page_size
    dec_keys = dec_pages.shape[1] * page_size
    dec_count = dec_pages.shape[0]
    tile = 4 * block_rows
    width = w_query.shape[0]
    same, other = rope_tables(positions)
    number = pl.BlockSpec(memory_space=pltpu.SMEM)
    array = pl.BlockSpec(memory_space=pltpu.VMEM)
    apart = pl.BlockSpec(memory_space=pl.ANY)
    flops = 2 * rows * (3 * HD * width + 2 * HD * (pre_keys + rows))
    return pl.pallas_call(
        functools.partial(attention_kernel, layout, block_rows, tile),
        out_shape=(
            jax.ShapeDtypeStruct((rows, HD), jnp.bfloat16),
            jax.ShapeDtypeStruct((2, rows, HD), jnp.bfloat16),
        ),
        in_specs=[number] * 5 + [apart] * (len(blocks) + 2) + [array] * 2 + [apart] * 3,
        out_specs=(array, array),
        scratch_shapes=[
            pltpu.VMEM((rows, width), jnp.bfloat16),
            pltpu.VMEM((width, 3 * HD), jnp.bfloat16),
            pltpu.VMEM((rows, HD), jnp.bfloat16),
            pltpu.VMEM((HD + 16, pre_keys + rows), jnp.bfloat16),
            pltpu.VMEM((pre_keys, HD), jnp.bfloat16),
            pltpu.VMEM((pre_keys, HD), jnp.bfloat16),
            pltpu.VMEM((dec_count, dec_keys, HD), jnp.bfloat16),
            pltpu.VMEM((dec_count, dec_keys, HD), jnp.bfloat16),
            pltpu.SemaphoreType.DMA((len(blocks),)),
            pltpu.SemaphoreType.DMA((3,)),
            pltpu.SemaphoreType.DMA((2,)),
            pltpu.SemaphoreType.DMA((2, dec_count)),
        ],
        compiler_params=pltpu.CompilerParams(vmem_limit_bytes=48 * MIB),
        cost_estimate=pl.CostEstimate(
            flops=flops, bytes_accessed=20 * MIB, transcendentals=rows * (pre_keys + rows)
        ),
        name="attention",
    )(
        place,
        pre_pos,
        dec_len,
        dec_pages,
        pre_pages,
        *blocks,
        w_query,
        w_keyval,
        same,
        other,
        k_pool,
        v_pool,
        earlier,
    )


def project_kernel(count, *refs):
    heads, weights = refs[:count], refs[count : 2 * count]
    own_ref, other_ref = refs[2 * count :]
    width = weights[0].shape[1]
    rows = own_ref.shape[0]
    step = math.gcd(width, 512)
    for start in range(0, width, step):
        here = slice(start, start + step)
        total = 0.0
        for first in range(0, count, 2):
            left = jnp.concatenate([heads[first][...], heads[first + 1][...]], axis=1)
            right = jnp.concatenate(
                [weights[first][:, here], weights[first + 1][:, here]], axis=0
            )
            total = total + jnp.dot(left, right, preferred_element_type=WIDE)
        own_ref[:, here] = total[:rows]
        other_ref[:, here] = total[rows:].astype(jnp.bfloat16)


def project(heads, weights, rows):
    array = pl.BlockSpec(memory_space=pltpu.VMEM)
    count, all_rows, width = len(heads), heads[0].shape[0], weights[0].shape[1]
    return pl.pallas_call(
        functools.partial(project_kernel, count),
        out_shape=(
            jax.ShapeDtypeStruct((rows, width), WIDE),
            jax.ShapeDtypeStruct((all_rows - rows, width), jnp.bfloat16),
        ),
        in_specs=[array] * (2 * count),
        out_specs=(array, array),
        compiler_params=pltpu.CompilerParams(vmem_limit_bytes=32 * MIB),
        cost_estimate=pl.CostEstimate(
            flops=2 * all_rows * width * count * HD, bytes_accessed=4 * MIB, transcendentals=0
        ),
        name="project",
    )(*heads, *weights)


def close_kernel(hidden_ref, gain_ref, *refs):
    *terms, residual_ref, normed_ref = refs
    total = hidden_ref[...].astype(WIDE)
    for term in terms:
        total = total + term[...].astype(WIDE)
    rounded = total.astype(jnp.bfloat16)
    residual_ref[...] = rounded
    total = rounded.astype(WIDE)
    factor = lax.rsqrt(jnp.mean(total * total, axis=1, keepdims=True) + EPSILON)
    normed_ref[...] = (total * factor * gain_ref[...]).astype(jnp.bfloat16)


def close(hidden, gain, terms):
    array = pl.BlockSpec(memory_space=pltpu.VMEM)
    return pl.pallas_call(
        close_kernel,
        out_shape=(jax.ShapeDtypeStruct(hidden.shape, jnp.bfloat16),) * 2,
        in_specs=[array] * (2 + len(terms)),
        out_specs=(array, array),
        compiler_params=pltpu.CompilerParams(vmem_limit_bytes=16 * MIB),
        name="close",
    )(hidden, gain[None, :], *terms)


def norm_kernel(hidden_ref, gain_ref, out_ref):
    values = hidden_ref[...].astype(WIDE)
    factor = lax.rsqrt(jnp.mean(values * values, axis=1, keepdims=True) + EPSILON)
    out_ref[...] = (values * factor * gain_ref[...]).astype(jnp.bfloat16)


def norm(hidden, gain):
    array = pl.BlockSpec(memory_space=pltpu.VMEM)
    return pl.pallas_call(
        norm_kernel,
        out_shape=jax.ShapeDtypeStruct(hidden.shape, jnp.bfloat16),
        in_specs=[array, array],
        out_specs=array,
        compiler_params=pltpu.CompilerParams(vmem_limit_bytes=16 * MIB),
        name="norm",
    )(hidden, gain[None, :])


def gather_blocks(rows, first):
    half = rows.shape[0] // 2
    from_x, from_y = swap(rows, 2), swap(rows, 4)
    beside = swap(after(rows, from_x), 1)
    x_1, y_2 = after((from_x[:half], from_y[half:]), *first)
    far = jnp.concatenate([swap(x_1, 4), swap(y_2, 2)], axis=0)
    near = jnp.concatenate([from_x, from_y], axis=0)
    near_beside = swap(near, 1)
    return (
        [[rows, beside], [near], [near_beside], [far, swap(far, 1)]],
        [[0, 1], [2, 4], [3, 5], [6, 7]],
    )


def gate_table(expert_ids, gates):
    req_count = lax.axis_size("req")
    exp_count = lax.axis_size("exp")
    experts = req_count * exp_count // SPLIT
    named = expert_ids.T[None] == jnp.arange(experts, dtype=jnp.int32)[:, None, None]
    table = jnp.sum(jnp.where(named, gates.T[None], 0.0), axis=1)
    near = jnp.stack([table, shift(table, 1)])
    near = jnp.concatenate([near, shift(near, 2)])
    bits = jnp.arange(0, exp_count, 2, dtype=jnp.int32)
    owner = lax.axis_index("req") * exp_count + (lax.axis_index("exp") ^ bits)
    chosen = (owner // SPLIT)[:, None] == jnp.arange(experts, dtype=jnp.int32)
    mine = jnp.sum(jnp.where(chosen[None, :, :, None], near[:, None], 0.0), axis=2)
    mine = jnp.pad(mine, ((0, 0), (0, -mine.shape[1] % 8), (0, 0)))
    marks = (mine > 0).astype(jnp.int32)
    return mine, jnp.cumsum(marks, axis=2) - marks


def deliver(buffer):
    result = lax.all_to_all(buffer, ("req", "exp"), split_axis=0, concat_axis=0, tiled=True)
    return result


def bring_back(buffer):
    result = lax.all_to_all(buffer, ("req", "exp"), split_axis=0, concat_axis=0, tiled=True)
    return result


def slots_of(choices, experts):
    return 2 * ((choices * 5 + 8 * experts - 1) // (8 * experts))


def sparse_experts(normed_moe, expert_ids, gates, w_in, w_down):
    local_rows, width = normed_moe.shape
    devices = lax.axis_size("req") * lax.axis_size("exp")
    experts = devices // SPLIT
    top = expert_ids.shape[1]
    capacity = slots_of(local_rows * top, experts)
    assigned = expert_ids.reshape(-1)
    count_all = assigned.shape[0]
    marks = (assigned[:, None] == jnp.arange(experts, dtype=jnp.int32)[None, :]).astype(jnp.int32)
    earlier = jnp.cumsum(marks, axis=0) - marks
    place = jnp.sum(earlier * marks, axis=1)
    target = assigned * capacity + place
    owner_rows = jnp.arange(count_all, dtype=jnp.int32) // top
    outgoing = (
        jnp.zeros((experts * capacity, width), jnp.bfloat16).at[target].set(normed_moe[owner_rows])
    )
    doubled = jnp.broadcast_to(
        outgoing.reshape(experts, 1, capacity, width), (experts, SPLIT, capacity, width)
    ).reshape(devices, capacity, width)
    arrived = deliver(doubled)
    piece_units = w_down.shape[1]
    inner = jnp.dot(
        arrived.reshape(devices * capacity, width), w_in[0], preferred_element_type=jnp.float32
    )
    activated = (jax.nn.silu(inner[:, :piece_units]) * inner[:, piece_units:]).astype(jnp.bfloat16)
    partial_value = (
        jnp.dot(activated, w_down[0], preferred_element_type=jnp.float32)
        .astype(jnp.bfloat16)
        .reshape(devices, capacity, width)
    )
    returned = bring_back(partial_value).reshape(devices * capacity, width)
    base_index = assigned * (SPLIT * capacity) + place
    lower_half = returned[base_index].astype(jnp.float32)
    upper_half = returned[base_index + capacity].astype(jnp.float32)
    weighted = (lower_half + upper_half) * gates.reshape(-1)[:, None]
    moe_out = jnp.sum(weighted.reshape(local_rows, top, width), axis=1)
    return moe_out


def body(
    hidden,
    attn_gain,
    w_query,
    w_keyval,
    k_pool,
    v_pool,
    dec_len,
    dec_pages,
    pre_pos,
    pre_pages,
    w_out,
    moe_gain,
    expert_ids,
    router_logits,
    w_in,
    w_down,
):
    local_rows, width = hidden.shape
    exp_count = lax.axis_size("exp")
    group_rows = local_rows * exp_count
    dec_count = dec_len.shape[0]
    quick = exp_count == 8
    experts = lax.axis_size("req") * exp_count // SPLIT
    capacity = slots_of(local_rows * expert_ids.shape[1], experts)
    normed_attn = norm(hidden, attn_gain)
    row_index = jnp.arange(group_rows, dtype=jnp.int32)
    own_positions = jnp.sum(
        jnp.where(row_index[:, None] == jnp.arange(dec_count), dec_len[None, :], 0), axis=1
    )
    positions = jnp.where(row_index < dec_count, own_positions, pre_pos[0] + row_index - dec_count)
    if quick:
        place = lax.axis_index("exp").reshape(1)
        gates = jax.nn.softmax(router_logits, axis=-1)
        near_gates, near_places = gate_table(expert_ids, gates)
        own_in, own_down = w_in[0], w_down[0]
        pair_in = swap(own_in, 1)
        groups, names = gather_blocks(normed_attn, (near_places, pair_in))
        far, late = groups[-1]
        own_out, late_down = after(w_out, far), after(own_down, late)
        out_blocks = [w_out] + [swap(own_out, bits) for bits in (2, 4, 6)]
        pieces = [(own_in, own_down), (pair_in, swap(late_down, 1))]
        earlier = near_places
    else:
        place = jnp.zeros((1,), jnp.int32)
        earlier = place
        blocks = jnp.split(lax.all_gather(normed_attn, "exp", axis=0, tiled=True), exp_count)
        groups = [blocks[at : at + 2] for at in range(0, exp_count, 2)]
        names = [[at, at + 1] for at in range(0, exp_count, 2)]
        out_blocks = jnp.split(lax.all_gather(w_out, "exp", axis=0, tiled=True), exp_count)
    attended, new_kv = attention(
        place,
        groups,
        names,
        (w_query, w_keyval),
        positions,
        (k_pool, v_pool),
        (pre_pos, dec_len, dec_pages, pre_pages),
        earlier,
    )
    if quick:
        attended = after(attended, pieces[1])
        pairs = jnp.split(attended, exp_count // 2)
        heads = [pairs[0]] + [swap(pairs[at], 2 * at) for at in range(1, exp_count // 2)]
        own, other = project(heads, out_blocks, local_rows)
        residual, normed_moe = close(hidden, moe_gain, [own, swap(other, 1)])
        mixed = plane_experts(
            normed_moe, residual, near_gates, near_places, pieces, capacity
        )
    else:
        heads = jnp.split(
            lax.all_to_all(attended, "exp", split_axis=0, concat_axis=0, tiled=True), exp_count
        )
        own, _ = project([jnp.tile(head, (2, 1)) for head in heads], out_blocks, local_rows)
        residual, normed_moe = close(hidden, moe_gain, [own])
        gates = jax.nn.softmax(router_logits, axis=-1)
        moe_out = sparse_experts(normed_moe, expert_ids, gates, w_in, w_down)
        mixed = (residual.astype(jnp.float32) + moe_out).astype(jnp.bfloat16)
    return (mixed, new_kv)


def solution(mesh):
    placed = (
        P(("req", "exp"), None),
        P(),
        P(None, "exp"),
        P(None, None, "exp"),
        P("req", None, "exp"),
        P("req", None, "exp"),
        P("req"),
        P("req", None),
        P("req"),
        P("req", None),
        P("exp", None),
        P(),
        P(("req", "exp"), None),
        P(("req", "exp"), None),
        P(("req", "exp"), None, None),
        P(("req", "exp"), None, None),
    )
    return jax.shard_map(
        body,
        mesh=mesh,
        in_specs=placed,
        out_specs=(P(("req", "exp"), None), P(None, "req", "exp")),
        check_vma=False,
    )
```

```python
import functools
import math

import jax
import jax.numpy as jnp
from jax import lax
from jax.experimental import pallas as pl
from jax.experimental.pallas import tpu as pltpu
from jax.sharding import PartitionSpec as P

HD = 128
SPLIT = 2


EPSILON = 1e-05
THETA = 10000.0


WIDE = jnp.float32


def swap(values, bits):
    count = lax.axis_size("exp")
    return lax.ppermute(values, "exp", [(d, d ^ bits) for d in range(count)])


def shift(values, steps):
    count = lax.axis_size("req")
    return lax.ppermute(values, "req", [(d, (d + steps) % count) for d in range(count)])


def after(values, *others):
    return lax.optimization_barrier((values, *others))[0]


def experts_kernel(part, wide, *refs):
    blocks, (own_in, own_down, pair_in, pair_down) = refs[:4], refs[4:8]
    outs = refs[8:12]
    rows_s, in_s, down_s, active_s, made_s, block_sem, in_sem, down_sem, out_sem = refs[12:]
    units, width = own_down.shape
    size = blocks[0].shape[0]
    parts, tiles = units // part, width // wide

    loads = [
        pltpu.make_async_copy(block, rows_s.at[pl.ds(at * size, size)], block_sem.at[at])
        for at, block in enumerate(blocks)
    ]
    arrivals = []
    for piece, weight in enumerate((own_in, pair_in)):
        for at in range(parts):
            number = piece * parts + at
            here = pl.ds(number * 2 * part, part), pl.ds((number * 2 + 1) * part, part)
            arrivals.append(
                [
                    pltpu.make_async_copy(
                        weight.at[:, pl.ds(half * units + at * part, part)],
                        in_s.at[:, here[half]],
                        in_sem.at[2 * number + half],
                    )
                    for half in range(2)
                ]
            )
    downs = [
        pltpu.make_async_copy(weight, down_s.at[pl.ds(piece * units, units)], down_sem.at[piece])
        for piece, weight in enumerate((own_down, pair_down))
    ]
    for copy in loads:
        copy.start()
    for pair in arrivals:
        for copy in pair:
            copy.start()
    for copy in downs:
        copy.start()
    for copy in loads:
        copy.wait()
    rows = rows_s[...]
    for number, pair in enumerate(arrivals):
        for copy in pair:
            copy.wait()
        both = jnp.dot(
            rows,
            in_s[:, 2 * part * number : 2 * part * (number + 1)],
            preferred_element_type=WIDE,
        )
        gate, up = both[:, :part], both[:, part:]
        active = gate / (1.0 + jnp.exp(-gate)) * up
        active_s[:, part * number : part * (number + 1)] = active.astype(jnp.bfloat16)
    for copy in downs:
        copy.wait()
    active = active_s[...]
    stores = []
    for tile in range(tiles):
        here = slice(tile * wide, (tile + 1) * wide)
        made = jnp.dot(active, down_s[:, here], preferred_element_type=WIDE)
        for at, out in enumerate(outs):
            mine = slice(at * size, (at + 1) * size)
            made_s[mine, here] = made[mine].astype(jnp.bfloat16)
            copy = pltpu.make_async_copy(
                made_s.at[pl.ds(at * size, size), pl.ds(tile * wide, wide)],
                out.at[:, pl.ds(tile * wide, wide)],
                out_sem.at[tile * len(outs) + at],
            )
            copy.start()
            stores.append(copy)
    for copy in stores:
        copy.wait()


def expert_rows(blocks, pieces):
    (own_in, own_down), (pair_in, pair_down) = pieces
    units, width = own_down.shape
    size, count = blocks[0].shape[0], len(blocks)
    rows = size * count
    part, wide = math.gcd(units, 256), math.gcd(width, 512)
    apart = pl.BlockSpec(memory_space=pl.ANY)
    return pl.pallas_call(
        functools.partial(experts_kernel, part, wide),
        out_shape=[jax.ShapeDtypeStruct((size, width), jnp.bfloat16)] * count,
        in_specs=[apart] * (count + 4),
        out_specs=[apart] * count,
        scratch_shapes=[
            pltpu.VMEM((rows, width), jnp.bfloat16),
            pltpu.VMEM((width, 4 * units), jnp.bfloat16),
            pltpu.VMEM((2 * units, width), jnp.bfloat16),
            pltpu.VMEM((rows, 2 * units), jnp.bfloat16),
            pltpu.VMEM((rows, width), jnp.bfloat16),
            pltpu.SemaphoreType.DMA((count,)),
            pltpu.SemaphoreType.DMA((4 * (units // part),)),
            pltpu.SemaphoreType.DMA((2,)),
            pltpu.SemaphoreType.DMA((count * (width // wide),)),
        ],
        compiler_params=pltpu.CompilerParams(vmem_limit_bytes=30 * MIB),
        cost_estimate=pl.CostEstimate(
            flops=12 * rows * width * units,
            bytes_accessed=16 * MIB,
            transcendentals=2 * rows * units,
        ),
        name="experts",
    )(*blocks, own_in, own_down, pair_in, pair_down)


def pick_kernel(gate_ref, place_ref, rows_ref, *refs):
    outs, (made_s, sem) = refs[:-2], refs[-2:]
    rows = rows_ref[...]
    capacity = outs[0].shape[0]
    stores = []
    for at, out in enumerate(outs):
        room = lax.broadcasted_iota(jnp.int32, (capacity, rows.shape[0]), 0)
        chosen = jnp.logical_and(gate_ref[at : at + 1, :] > 0, place_ref[at : at + 1, :] == room)
        picked = jnp.where(chosen, 1.0, 0.0).astype(jnp.bfloat16)
        made = jnp.dot(picked, rows, preferred_element_type=WIDE).astype(jnp.bfloat16)
        made_s[at * capacity : (at + 1) * capacity, :] = made
        copy = pltpu.make_async_copy(
            made_s.at[pl.ds(at * capacity, capacity)], out, sem.at[at]
        )
        copy.start()
        stores.append(copy)
    for copy in stores:
        copy.wait()


def pick(rows, gates, places, count, capacity):
    array = pl.BlockSpec(memory_space=pltpu.VMEM)
    width = rows.shape[1]
    return pl.pallas_call(
        pick_kernel,
        out_shape=[jax.ShapeDtypeStruct((capacity, width), jnp.bfloat16)] * count,
        in_specs=[array] * 3,
        out_specs=[pl.BlockSpec(memory_space=pl.ANY)] * count,
        scratch_shapes=[
            pltpu.VMEM((count * capacity, width), jnp.bfloat16),
            pltpu.SemaphoreType.DMA((count,)),
        ],
        compiler_params=pltpu.CompilerParams(vmem_limit_bytes=12 * MIB),
        cost_estimate=pl.CostEstimate(
            flops=2 * count * capacity * rows.size, bytes_accessed=MIB, transcendentals=0
        ),
        name="pick",
    )(gates, places, rows)


def merge_kernel(count, gate_ref, place_ref, *refs):
    parts, terms, (out_ref, parts_s, sem) = refs[:count], refs[count:-3], refs[-3:]
    capacity = parts[0].shape[0]
    loads = []
    for at, part in enumerate(parts):
        here = parts_s.at[pl.ds(at * capacity, capacity)]
        loads.append(pltpu.make_async_copy(part, here, sem.at[at]))
        loads[-1].start()
    gates, places = gate_ref[...].T, place_ref[...].T
    total = 0.0
    for at in range(count):
        gate, place = gates[:, at : at + 1], places[:, at : at + 1]
        room = lax.broadcasted_iota(jnp.int32, (gates.shape[0], capacity), 1)
        chosen = jnp.logical_and(gate > 0, place == room)
        spread = jnp.where(chosen, 1.0, 0.0).astype(jnp.bfloat16)
        loads[at].wait()
        part = parts_s[at * capacity : (at + 1) * capacity, :]
        total = total + gate * jnp.dot(spread, part, preferred_element_type=WIDE)
    for term in terms:
        total = total + term[...].astype(WIDE)
    out_ref[...] = total.astype(jnp.bfloat16)


def merge(parts, gates, places, terms):
    array = pl.BlockSpec(memory_space=pltpu.VMEM)
    count, (capacity, width) = len(parts), parts[0].shape
    rows = gates.shape[1]
    return pl.pallas_call(
        functools.partial(merge_kernel, count),
        out_shape=jax.ShapeDtypeStruct((rows, width), jnp.bfloat16),
        in_specs=[array] * 2
        + [pl.BlockSpec(memory_space=pl.ANY)] * count
        + [array] * len(terms),
        out_specs=array,
        scratch_shapes=[
            pltpu.VMEM((count * capacity, width), jnp.bfloat16),
            pltpu.SemaphoreType.DMA((count,)),
        ],
        compiler_params=pltpu.CompilerParams(vmem_limit_bytes=16 * MIB),
        cost_estimate=pl.CostEstimate(
            flops=2 * rows * width * count * capacity, bytes_accessed=MIB, transcendentals=0
        ),
        name="merge",
    )(gates, places, *parts, *terms)


def plane_experts(normed_moe, residual, gates, places, pieces, capacity):
    steps = lax.axis_size("req")
    count = lax.axis_size("exp") // 2
    def exchange(parts, *earlier):
        mine, *others = parts
        others = after(tuple(others), *earlier)
        return [mine, *(swap(part, 2 * at) for at, part in enumerate(others, 1))]

    def use(step):
        return pick(moved[step], gates[step], places[step], count, capacity)

    moved = [normed_moe]
    came = [exchange(use(0))]
    made, back, chain = [], [], []
    for step in range(1, steps):
        moved.append(shift(moved[-1], 1))
        if step == 1:
            moved[1] = after(moved[1], came[0])
    for step in range(1, steps):
        made.append(expert_rows(after(came[step - 1], *made[-1:]), pieces))
        if step > 2:
            back.append(exchange(made[step - 2]))
        came.append(exchange(use(step), *came[step - 2 : step - 1]))
    made.append(expert_rows(after(came[-1], made[-1]), pieces))
    for step in range(1, steps):
        if step >= len(back) + 1:
            back.append(exchange(made[step], *back[step - 2 : step - 1]))
        chain = [merge(back[step - 1], gates[step], places[step], chain)]
        chain = [shift(chain[0], 1)]
    last = exchange(made[0], *back[-2:-1])
    return merge(last, gates[0], places[0], [*chain, residual])


LOW = -1e30
MIB = 1 << 20


def rope_tables(positions):
    half = HD // 2
    steps = jnp.arange(half, dtype=WIDE)
    frequency = jnp.exp(steps * (-2.0 * math.log(THETA) / HD))
    angles = positions.astype(WIDE)[:, None] * frequency[None, :]
    cosine, sine = jnp.cos(angles), jnp.sin(angles)
    return (
        jnp.concatenate([cosine, cosine], axis=1),
        jnp.concatenate([-sine, sine], axis=1),
    )


def dot_rows(left, right):
    return lax.dot_general(left, right, (((1,), (1,)), ((), ())), preferred_element_type=WIDE)


def attention_kernel(layout, block_rows, tile, *refs):
    ref_count = sum(count for count, _ in layout)
    place_ref, length_ref, limits_ref, dec_pages_ref, pre_pages_ref = refs[:5]
    sources = refs[5 : 5 + ref_count]
    w_query, w_keyval, same_ref, other_ref, k_pool, v_pool, _, out_ref, kv_ref = refs[
        5 + ref_count : 14 + ref_count
    ]
    (rows_s, weight_s, query_s, turned_s, pre_k, pre_v, dec_k, dec_v) = refs[
        14 + ref_count : 22 + ref_count
    ]
    row_sem, weight_sem, pre_sem, dec_sem = refs[22 + ref_count :]
    page_size = k_pool.shape[1]
    dec_count, dec_pages = dec_pages_ref.shape
    pre_pages = pre_pages_ref.shape[1]
    pre_keys = pre_pages * page_size
    rows = query_s.shape[0]
    dec_keys = dec_pages * page_size
    place = place_ref[0]
    length = length_ref[0]
    rate = math.log2(math.e) / math.sqrt(HD)

    weight_copies = [
        pltpu.make_async_copy(part, weight_s.at[:, pl.ds(at * HD, HD)], weight_sem.at[at])
        for at, part in enumerate((w_query, w_keyval.at[0], w_keyval.at[1]))
    ]
    row_copies, start = [], 0
    for at, source in enumerate(sources):
        here = rows_s.at[pl.ds(start, source.shape[0])]
        row_copies.append(pltpu.make_async_copy(source, here, row_sem.at[at]))
        start += source.shape[0]
    for copy in weight_copies + row_copies:
        copy.start()

    def fetch_prefix(at, carry):
        page = pre_pages_ref[0, at]
        here = pl.ds(pl.multiple_of(at * page_size, page_size), page_size)
        pltpu.make_async_copy(k_pool.at[page], pre_k.at[here], pre_sem.at[0]).start()
        pltpu.make_async_copy(v_pool.at[page], pre_v.at[here], pre_sem.at[1]).start()
        return carry

    lax.fori_loop(0, pre_pages, fetch_prefix, 0)
    for request in range(dec_count):

        def fetch_decode(at, carry):
            page = dec_pages_ref[request, at]
            here = pl.ds(pl.multiple_of(at * page_size, page_size), page_size)
            pltpu.make_async_copy(
                k_pool.at[page], dec_k.at[request, here], dec_sem.at[0, request]
            ).start()
            pltpu.make_async_copy(
                v_pool.at[page], dec_v.at[request, here], dec_sem.at[1, request]
            ).start()
            return carry

        lax.fori_loop(0, dec_pages, fetch_decode, 0)

    for copy in weight_copies:
        copy.wait()
    start = 0
    for count, names in layout:
        for _ in range(count):
            row_copies.pop(0).wait()
        size = block_rows * len(names)
        made = jnp.dot(rows_s[start : start + size], weight_s[...], preferred_element_type=WIDE)
        start += size
        for at, name in enumerate(names):
            mine = made[at * block_rows : (at + 1) * block_rows]
            first = pl.multiple_of((place ^ name) * block_rows, block_rows)
            here = pl.ds(first, block_rows)
            same, other = same_ref[here, :], other_ref[here, :]
            query, key = mine[:, :HD], mine[:, HD : 2 * HD]
            query_s[here, :] = (query * same + pltpu.roll(query, HD // 2, 1) * other).astype(
                jnp.bfloat16
            )
            kv_ref[0, here, :] = (key * same + pltpu.roll(key, HD // 2, 1) * other).astype(
                jnp.bfloat16
            )
            kv_ref[1, here, :] = mine[:, 2 * HD :].astype(jnp.bfloat16)

    pltpu.make_async_copy(pre_k, pre_k, pre_sem.at[0]).wait()
    pltpu.make_async_copy(pre_v, pre_v, pre_sem.at[1]).wait()

    turned_s[:HD, :pre_keys] = pre_v[...].T
    turned_s[:HD, pre_keys:] = kv_ref[1].T
    turned_s[HD:, :] = jnp.ones((turned_s.shape[0] - HD, turned_s.shape[1]), jnp.bfloat16)
    slots = lax.broadcasted_iota(jnp.int32, (pre_keys, 1), 0)
    bias = jnp.where(slots < length, 0.0, LOW)
    for at in range(rows // tile):
        start = at * tile
        held = start + tile
        query = query_s[start:held, :]
        scores = dot_rows(pre_k[...], query) * rate + bias
        own = dot_rows(kv_ref[0, :held, :], query) * rate
        seen = lax.broadcasted_iota(jnp.int32, own.shape, 0)
        asked = start + lax.broadcasted_iota(jnp.int32, own.shape, 1)
        own = jnp.where(jnp.logical_and(seen >= dec_count, seen <= asked), own, LOW)
        highest = jnp.maximum(
            jnp.max(scores, axis=0, keepdims=True), jnp.max(own, axis=0, keepdims=True)
        )
        weights = jnp.exp2(scores - highest).astype(jnp.bfloat16)
        own_weights = jnp.exp2(own - highest).astype(jnp.bfloat16)
        total = jnp.dot(
            turned_s[:, :pre_keys], weights, preferred_element_type=WIDE
        ) + jnp.dot(
            turned_s[:, pre_keys : pre_keys + held], own_weights, preferred_element_type=WIDE
        )
        done = (total[:HD] / total[HD : HD + 1]).T.astype(jnp.bfloat16)
        for part in range(tile // block_rows):
            target = (at * (tile // block_rows) + part) ^ place
            target = pl.multiple_of(target * block_rows, block_rows)
            out_ref[pl.ds(target, block_rows), :] = done[
                part * block_rows : (part + 1) * block_rows
            ]

    few = 16
    query = query_s[:few, :]
    row = lax.broadcasted_iota(jnp.int32, (few, HD), 0)
    own_scores = dot_rows(query, kv_ref[0, :few, :]) * rate
    first_rows = pl.ds(pl.multiple_of(place * block_rows, block_rows), few)
    result = out_ref[first_rows, :].astype(WIDE)
    for request in range(dec_count):
        pltpu.make_async_copy(dec_k.at[request], dec_k.at[request], dec_sem.at[0, request]).wait()
        pltpu.make_async_copy(dec_v.at[request], dec_v.at[request], dec_sem.at[1, request]).wait()
        scores = dot_rows(query, dec_k[request]) * rate
        slots = lax.broadcasted_iota(jnp.int32, (few, dec_keys), 1)
        scores = jnp.where(slots < limits_ref[request], scores, LOW)
        itself = lax.broadcasted_iota(jnp.int32, (few, few), 1) == request
        own = jnp.where(itself, own_scores, LOW)
        highest = jnp.maximum(
            jnp.max(scores, axis=1, keepdims=True), jnp.max(own, axis=1, keepdims=True)
        )
        weights = jnp.exp2(scores - highest)
        own_weights = jnp.exp2(own - highest)
        total = jnp.sum(weights, axis=1, keepdims=True) + jnp.sum(
            own_weights, axis=1, keepdims=True
        )
        summed = jnp.dot(
            weights.astype(jnp.bfloat16), dec_v[request], preferred_element_type=WIDE
        ) + jnp.dot(
            own_weights.astype(jnp.bfloat16), kv_ref[1, :few, :], preferred_element_type=WIDE
        )
        result = jnp.where(row == request, summed / total, result)
    out_ref[first_rows, :] = result.astype(jnp.bfloat16)


def attention(place, groups, names, weights, positions, pools, tables, earlier):
    pre_pos, dec_len, dec_pages, pre_pages = tables
    k_pool, v_pool = pools
    w_query, w_keyval = weights
    blocks = [block for group in groups for block in group]
    rows = sum(block.shape[0] for block in blocks)
    block_rows = rows // sum(len(group) for group in names)
    layout = [(len(group), name) for group, name in zip(groups, names, strict=True)]
    page_size = k_pool.shape[1]
    pre_keys = pre_pages.shape[1] * page_size
    dec_keys = dec_pages.shape[1] * page_size
    dec_count = dec_pages.shape[0]
    tile = 4 * block_rows
    width = w_query.shape[0]
    same, other = rope_tables(positions)
    number = pl.BlockSpec(memory_space=pltpu.SMEM)
    array = pl.BlockSpec(memory_space=pltpu.VMEM)
    apart = pl.BlockSpec(memory_space=pl.ANY)
    flops = 2 * rows * (3 * HD * width + 2 * HD * (pre_keys + rows))
    return pl.pallas_call(
        functools.partial(attention_kernel, layout, block_rows, tile),
        out_shape=(
            jax.ShapeDtypeStruct((rows, HD), jnp.bfloat16),
            jax.ShapeDtypeStruct((2, rows, HD), jnp.bfloat16),
        ),
        in_specs=[number] * 5 + [apart] * (len(blocks) + 2) + [array] * 2 + [apart] * 3,
        out_specs=(array, array),
        scratch_shapes=[
            pltpu.VMEM((rows, width), jnp.bfloat16),
            pltpu.VMEM((width, 3 * HD), jnp.bfloat16),
            pltpu.VMEM((rows, HD), jnp.bfloat16),
            pltpu.VMEM((HD + 16, pre_keys + rows), jnp.bfloat16),
            pltpu.VMEM((pre_keys, HD), jnp.bfloat16),
            pltpu.VMEM((pre_keys, HD), jnp.bfloat16),
            pltpu.VMEM((dec_count, dec_keys, HD), jnp.bfloat16),
            pltpu.VMEM((dec_count, dec_keys, HD), jnp.bfloat16),
            pltpu.SemaphoreType.DMA((len(blocks),)),
            pltpu.SemaphoreType.DMA((3,)),
            pltpu.SemaphoreType.DMA((2,)),
            pltpu.SemaphoreType.DMA((2, dec_count)),
        ],
        compiler_params=pltpu.CompilerParams(vmem_limit_bytes=48 * MIB),
        cost_estimate=pl.CostEstimate(
            flops=flops, bytes_accessed=20 * MIB, transcendentals=rows * (pre_keys + rows)
        ),
        name="attention",
    )(
        place,
        pre_pos,
        dec_len,
        dec_pages,
        pre_pages,
        *blocks,
        w_query,
        w_keyval,
        same,
        other,
        k_pool,
        v_pool,
        earlier,
    )


def project_kernel(count, *refs):
    heads, weights = refs[:count], refs[count : 2 * count]
    own_ref, other_ref = refs[2 * count :]
    width = weights[0].shape[1]
    rows = own_ref.shape[0]
    step = math.gcd(width, 512)
    for start in range(0, width, step):
        here = slice(start, start + step)
        total = 0.0
        for first in range(0, count, 2):
            left = jnp.concatenate([heads[first][...], heads[first + 1][...]], axis=1)
            right = jnp.concatenate(
                [weights[first][:, here], weights[first + 1][:, here]], axis=0
            )
            total = total + jnp.dot(left, right, preferred_element_type=WIDE)
        own_ref[:, here] = total[:rows]
        other_ref[:, here] = total[rows:].astype(jnp.bfloat16)


def project(heads, weights, rows):
    array = pl.BlockSpec(memory_space=pltpu.VMEM)
    count, all_rows, width = len(heads), heads[0].shape[0], weights[0].shape[1]
    return pl.pallas_call(
        functools.partial(project_kernel, count),
        out_shape=(
            jax.ShapeDtypeStruct((rows, width), WIDE),
            jax.ShapeDtypeStruct((all_rows - rows, width), jnp.bfloat16),
        ),
        in_specs=[array] * (2 * count),
        out_specs=(array, array),
        compiler_params=pltpu.CompilerParams(vmem_limit_bytes=32 * MIB),
        cost_estimate=pl.CostEstimate(
            flops=2 * all_rows * width * count * HD, bytes_accessed=4 * MIB, transcendentals=0
        ),
        name="project",
    )(*heads, *weights)


def close_kernel(hidden_ref, gain_ref, *refs):
    *terms, residual_ref, normed_ref = refs
    total = hidden_ref[...].astype(WIDE)
    for term in terms:
        total = total + term[...].astype(WIDE)
    rounded = total.astype(jnp.bfloat16)
    residual_ref[...] = rounded
    total = rounded.astype(WIDE)
    factor = lax.rsqrt(jnp.mean(total * total, axis=1, keepdims=True) + EPSILON)
    normed_ref[...] = (total * factor * gain_ref[...]).astype(jnp.bfloat16)


def close(hidden, gain, terms):
    array = pl.BlockSpec(memory_space=pltpu.VMEM)
    return pl.pallas_call(
        close_kernel,
        out_shape=(jax.ShapeDtypeStruct(hidden.shape, jnp.bfloat16),) * 2,
        in_specs=[array] * (2 + len(terms)),
        out_specs=(array, array),
        compiler_params=pltpu.CompilerParams(vmem_limit_bytes=16 * MIB),
        name="close",
    )(hidden, gain[None, :], *terms)


def norm_kernel(hidden_ref, gain_ref, out_ref):
    values = hidden_ref[...].astype(WIDE)
    factor = lax.rsqrt(jnp.mean(values * values, axis=1, keepdims=True) + EPSILON)
    out_ref[...] = (values * factor * gain_ref[...]).astype(jnp.bfloat16)


def norm(hidden, gain):
    array = pl.BlockSpec(memory_space=pltpu.VMEM)
    return pl.pallas_call(
        norm_kernel,
        out_shape=jax.ShapeDtypeStruct(hidden.shape, jnp.bfloat16),
        in_specs=[array, array],
        out_specs=array,
        compiler_params=pltpu.CompilerParams(vmem_limit_bytes=16 * MIB),
        name="norm",
    )(hidden, gain[None, :])


def gather_blocks(rows, first, second):
    half = rows.shape[0] // 2
    from_x, from_y = swap(rows, 2), swap(rows, 4)
    beside = swap(after(rows, from_x), 1)
    x_1, y_2 = after((from_x[:half], from_y[half:]), *first)
    far = jnp.concatenate([swap(x_1, 4), swap(y_2, 2)], axis=0)
    near = jnp.concatenate([from_x, from_y], axis=0)
    near_beside = swap(near, 1)
    return (
        [[rows, beside], [near], [near_beside], [far, swap(after(far, second), 1)]],
        [[0, 1], [2, 4], [3, 5], [6, 7]],
    )


def gate_table(expert_ids, gates):
    req_count = lax.axis_size("req")
    exp_count = lax.axis_size("exp")
    experts = req_count * exp_count // SPLIT
    named = expert_ids.T[None] == jnp.arange(experts, dtype=jnp.int32)[:, None, None]
    table = jnp.sum(jnp.where(named, gates.T[None], 0.0), axis=1)
    near = jnp.stack([table, shift(table, 1)])
    near = jnp.concatenate([near, shift(near, 2)])
    bits = jnp.arange(0, exp_count, 2, dtype=jnp.int32)
    owner = lax.axis_index("req") * exp_count + (lax.axis_index("exp") ^ bits)
    chosen = (owner // SPLIT)[:, None] == jnp.arange(experts, dtype=jnp.int32)
    mine = jnp.sum(jnp.where(chosen[None, :, :, None], near[:, None], 0.0), axis=2)
    mine = jnp.pad(mine, ((0, 0), (0, -mine.shape[1] % 8), (0, 0)))
    marks = (mine > 0).astype(jnp.int32)
    return mine, jnp.cumsum(marks, axis=2) - marks


def deliver(buffer):
    result = lax.all_to_all(buffer, ("req", "exp"), split_axis=0, concat_axis=0, tiled=True)
    return result


def bring_back(buffer):
    result = lax.all_to_all(buffer, ("req", "exp"), split_axis=0, concat_axis=0, tiled=True)
    return result


def slots_of(choices, experts):
    return 2 * ((choices * 5 + 8 * experts - 1) // (8 * experts))


def sparse_experts(normed_moe, expert_ids, gates, w_in, w_down):
    local_rows, width = normed_moe.shape
    devices = lax.axis_size("req") * lax.axis_size("exp")
    experts = devices // SPLIT
    top = expert_ids.shape[1]
    capacity = slots_of(local_rows * top, experts)
    assigned = expert_ids.reshape(-1)
    count_all = assigned.shape[0]
    marks = (assigned[:, None] == jnp.arange(experts, dtype=jnp.int32)[None, :]).astype(jnp.int32)
    earlier = jnp.cumsum(marks, axis=0) - marks
    place = jnp.sum(earlier * marks, axis=1)
    target = assigned * capacity + place
    owner_rows = jnp.arange(count_all, dtype=jnp.int32) // top
    outgoing = (
        jnp.zeros((experts * capacity, width), jnp.bfloat16).at[target].set(normed_moe[owner_rows])
    )
    doubled = jnp.broadcast_to(
        outgoing.reshape(experts, 1, capacity, width), (experts, SPLIT, capacity, width)
    ).reshape(devices, capacity, width)
    arrived = deliver(doubled)
    piece_units = w_down.shape[1]
    inner = jnp.dot(
        arrived.reshape(devices * capacity, width), w_in[0], preferred_element_type=jnp.float32
    )
    activated = (jax.nn.silu(inner[:, :piece_units]) * inner[:, piece_units:]).astype(jnp.bfloat16)
    partial_value = (
        jnp.dot(activated, w_down[0], preferred_element_type=jnp.float32)
        .astype(jnp.bfloat16)
        .reshape(devices, capacity, width)
    )
    returned = bring_back(partial_value).reshape(devices * capacity, width)
    base_index = assigned * (SPLIT * capacity) + place
    lower_half = returned[base_index].astype(jnp.float32)
    upper_half = returned[base_index + capacity].astype(jnp.float32)
    weighted = (lower_half + upper_half) * gates.reshape(-1)[:, None]
    moe_out = jnp.sum(weighted.reshape(local_rows, top, width), axis=1)
    return moe_out


def body(
    hidden,
    attn_gain,
    w_query,
    w_keyval,
    k_pool,
    v_pool,
    dec_len,
    dec_pages,
    pre_pos,
    pre_pages,
    w_out,
    moe_gain,
    expert_ids,
    router_logits,
    w_in,
    w_down,
):
    local_rows, width = hidden.shape
    exp_count = lax.axis_size("exp")
    group_rows = local_rows * exp_count
    dec_count = dec_len.shape[0]
    quick = exp_count == 8
    experts = lax.axis_size("req") * exp_count // SPLIT
    capacity = slots_of(local_rows * expert_ids.shape[1], experts)
    normed_attn = norm(hidden, attn_gain)
    row_index = jnp.arange(group_rows, dtype=jnp.int32)
    own_positions = jnp.sum(
        jnp.where(row_index[:, None] == jnp.arange(dec_count), dec_len[None, :], 0), axis=1
    )
    positions = jnp.where(row_index < dec_count, own_positions, pre_pos[0] + row_index - dec_count)
    if quick:
        place = lax.axis_index("exp").reshape(1)
        gates = jax.nn.softmax(router_logits, axis=-1)
        near_gates, near_places = gate_table(expert_ids, gates)
        own_in, own_down = w_in[0], w_down[0]
        pair_in = swap(own_in, 1)
        groups, names = gather_blocks(normed_attn, (pair_in,), near_places)
        far, late = groups[-1]
        own_out, late_down = after(w_out, far), after(own_down, late)
        out_blocks = [w_out] + [swap(own_out, bits) for bits in (2, 4, 6)]
        pieces = [(own_in, own_down), (pair_in, swap(late_down, 1))]
        earlier = near_places
    else:
        place = jnp.zeros((1,), jnp.int32)
        earlier = place
        blocks = jnp.split(lax.all_gather(normed_attn, "exp", axis=0, tiled=True), exp_count)
        groups = [blocks[at : at + 2] for at in range(0, exp_count, 2)]
        names = [[at, at + 1] for at in range(0, exp_count, 2)]
        out_blocks = jnp.split(lax.all_gather(w_out, "exp", axis=0, tiled=True), exp_count)
    attended, new_kv = attention(
        place,
        groups,
        names,
        (w_query, w_keyval),
        positions,
        (k_pool, v_pool),
        (pre_pos, dec_len, dec_pages, pre_pages),
        earlier,
    )
    if quick:
        attended = after(attended, pieces[1])
        pairs = jnp.split(attended, exp_count // 2)
        heads = [pairs[0]] + [swap(pairs[at], 2 * at) for at in range(1, exp_count // 2)]
        own, other = project(heads, out_blocks, local_rows)
        residual, normed_moe = close(hidden, moe_gain, [own, swap(other, 1)])
        mixed = plane_experts(
            normed_moe, residual, near_gates, near_places, pieces, capacity
        )
    else:
        heads = jnp.split(
            lax.all_to_all(attended, "exp", split_axis=0, concat_axis=0, tiled=True), exp_count
        )
        own, _ = project([jnp.tile(head, (2, 1)) for head in heads], out_blocks, local_rows)
        residual, normed_moe = close(hidden, moe_gain, [own])
        gates = jax.nn.softmax(router_logits, axis=-1)
        moe_out = sparse_experts(normed_moe, expert_ids, gates, w_in, w_down)
        mixed = (residual.astype(jnp.float32) + moe_out).astype(jnp.bfloat16)
    return (mixed, new_kv)


def solution(mesh):
    placed = (
        P(("req", "exp"), None),
        P(),
        P(None, "exp"),
        P(None, None, "exp"),
        P("req", None, "exp"),
        P("req", None, "exp"),
        P("req"),
        P("req", None),
        P("req"),
        P("req", None),
        P("exp", None),
        P(),
        P(("req", "exp"), None),
        P(("req", "exp"), None),
        P(("req", "exp"), None, None),
        P(("req", "exp"), None, None),
    )
    return jax.shard_map(
        body,
        mesh=mesh,
        in_specs=placed,
        out_specs=(P(("req", "exp"), None), P(None, "req", "exp")),
        check_vma=False,
    )
```
